512 devices in a mesh: gx: 4 (over x_hi, core), gy: 16 (over x_lo, y), ma: 8 (over z).
Axes of the slice: x: 4 (x_hi: 2, x_lo: 2; x = x_hi * 2 + x_lo), y: 8, z: 8, core: 2. Of those that a mesh axis runs over, the one named last changes fastest.
Arguments:
- spectra: bfloat16 [64, 2048, 2048], P('gx', 'gy', 'ma'), as said below
- loadings: float32 [32, 64, 2048], P(None, 'gx', 'gy'), as said below
- profiles: float32 [32, 2048], P(None, 'ma'), may hold values from 0.5 to 2
Outputs:
- new_load: float32 [32, 64, 2048], P(None, 'gx', 'gy')
- new_prof: float32 [32, 2048], P(None, 'ma')
The draws below stay inside these ranges and needn't reach their ends.
Inputs may be any that keep to these rules, and one draw needn't show every extreme that they name: `spectra`: positive. `loadings`: positive.
All inputs are finite; a program needn't handle non-finite values.
Results may differ from the reference program's by a relative error of at most 0.0003.
Values may be sent and summed in bfloat16 or wider, within the bound.
A program may use at most 64 MiB of HBM per device.

```python
import math
import jax
import jax.numpy as jnp
from jax import lax

CX = 16
CY = 128
M = 2048
K = 32
RADIUS = 2
NX = 64
NY = 2048


peak_count = 4


def region_index():
    across_y = NY // CY
    rows_x = jnp.arange(NX).astype(jnp.int32) // CX
    rows_y = jnp.arange(NY).astype(jnp.int32) // CY
    return rows_x[:, None] * across_y + rows_y[None, :]


def region_total():
    return NX // CX * (NY // CY)


def draw_spectra(key, part):
    key = jax.random.fold_in(key, 11)
    keys = jax.random.split(key, 5)
    count = region_total()
    slopes = jax.random.uniform(keys[0], (count, 1), jnp.float32, -2.0, 2.0)
    centers = jax.random.uniform(keys[1], (count, peak_count, 1), jnp.float32, 0.0, 1.0) * M
    heights = jnp.exp(jax.random.uniform(keys[2], (count, peak_count, 1), jnp.float32) * jnp.log(8.0))
    widths = (1.0 + jax.random.uniform(keys[3], (count, peak_count, 1), jnp.float32)) * (M / 64.0)
    mass = jnp.arange(M).astype(jnp.float32)
    scaled = (mass[None, None, :] - centers) / widths
    peaks = jnp.sum(heights * jnp.exp(-0.5 * scaled * scaled), axis=1)
    table = jnp.exp(slopes * mass[None, :] / M) * (1.0 + peaks)
    trend = table[region_index()]
    uniform_part = jax.random.uniform(keys[4], (NX, NY, M), jnp.float32)
    values = jnp.exp(jnp.log(0.1) + uniform_part * jnp.log(100.0))
    return (values * trend).astype(jnp.bfloat16)


def draw_loadings(key, part):
    key = jax.random.fold_in(key, 23)
    first, second = jax.random.split(key)
    count = region_total()
    levels = jnp.exp(jnp.log(0.25) + jax.random.uniform(first, (K, count), jnp.float32) * jnp.log(16.0))
    noise = jnp.exp(jnp.log(0.5) + jax.random.uniform(second, (K, NX, NY), jnp.float32) * jnp.log(4.0))
    return levels[:, region_index()] * noise


def block_scale(key, shape, cuts, low, high):
    level = 1.0
    for axis_at, parts in cuts:
        steps = jax.random.uniform(jax.random.fold_in(jax.random.fold_in(key, 6), axis_at), (parts,), jnp.float32, low / len(cuts), high / len(cuts))
        level = level * jnp.repeat(jnp.exp(steps), shape[axis_at] // parts).reshape((-1,) + (1,) * (len(shape) - 1 - axis_at))
    return level


def setup_inputs(seed: int = 0) -> dict:
    key_list = jax.random.split(jax.random.key(seed), 4)
    return {
        "spectra": draw_spectra(jax.random.fold_in(key_list[3], 71), 0),
        "loadings": draw_loadings(jax.random.fold_in(key_list[3], 71), 0),
        "profiles": jnp.clip(jnp.exp(math.log(2.0) - 1.3862944 * jax.random.uniform(key_list[2], (K, M), jnp.float32) ** block_scale(key_list[2], (K, M), ((1, 8),), -0.2, 0.2)), 0.5, 2.0),
    }


epsilon = 1e-6


def kernel_taps():
    offsets = jnp.arange(-RADIUS, RADIUS + 1).astype(jnp.float32)
    raw = jnp.exp(-offsets * offsets / 2.0)
    return raw / jnp.sum(raw)


def smooth_dim(padded, dim, count):
    taps = kernel_taps()
    total = None
    for offset in range(2 * RADIUS + 1):
        term = taps[offset] * lax.slice_in_dim(padded, offset, offset + count, axis=dim)
        total = term if total is None else total + term
    return total


def smooth_block(piece):
    width = RADIUS
    padded = jnp.pad(piece, ((width, width), (0, 0), (0, 0)))
    along_x = smooth_dim(padded, 0, piece.shape[0])
    padded = jnp.pad(along_x, ((0, 0), (width, width), (0, 0)))
    return smooth_dim(padded, 1, piece.shape[1])


def reference(spectra, loadings, profiles):
    block = min(128, M)
    nblocks = M // block
    indices = jnp.arange(nblocks).astype(jnp.int32)
    high = lax.Precision.HIGHEST

    def smoothed_at(index):
        piece = lax.dynamic_slice_in_dim(spectra, (index * block).astype(jnp.int32), block, 2)
        return smooth_block(piece.astype(jnp.float32))

    def add_background(carry, index):
        return carry + jnp.sum(smoothed_at(index), axis=2), None

    start = jnp.zeros((NX, NY), jnp.float32)
    total, unused = lax.scan(add_background, start, indices)
    background = total / M
    gram_load = jnp.einsum('kxy,jxy->kj', loadings, loadings, precision=high)

    def update_block(carry, index):
        numer_load, gram_prof = carry
        cleaned = jnp.maximum(smoothed_at(index) - background[:, :, None], 0.0)
        numer_prof = jnp.einsum('kxy,xym->km', loadings, cleaned, precision=high)
        old_prof = lax.dynamic_slice_in_dim(profiles, (index * block).astype(jnp.int32), block, 1)
        fresh = old_prof * numer_prof / (jnp.dot(gram_load, old_prof, precision=high) + epsilon)
        numer_load = numer_load + jnp.einsum('km,xym->kxy', fresh, cleaned, precision=high)
        gram_prof = gram_prof + jnp.dot(fresh, fresh.T, precision=high)
        return (numer_load, gram_prof), fresh

    init = (jnp.zeros((K, NX, NY), jnp.float32), jnp.zeros((K, K), jnp.float32))
    (numer_load, gram_prof), pieces = lax.scan(update_block, init, indices)
    new_prof = jnp.transpose(pieces, (1, 0, 2)).reshape(K, M)
    below = jnp.einsum('kj,jxy->kxy', gram_prof, loadings, precision=high) + epsilon
    new_load = loadings * numer_load / below
    return new_load, new_prof
```

```python
import functools

import jax
import jax.numpy as jnp
import ml_dtypes
import numpy as np
from jax import lax
from jax.experimental import pallas as pl
from jax.experimental.pallas import tpu as pltpu
from jax.sharding import PartitionSpec as P

MESH = pl.DeviceIdType.MESH
F32 = jnp.float32
BF16 = jnp.bfloat16
HIGH = lax.Precision.HIGHEST

RADIUS = 2
SIDE = 16
GROUP = 8
EPSILON = 1e-06
ORDER = (4, 3, 5, 2, 6, 1, 7)

NT = (((1,), (1,)), ((), ()))
NN = (((1,), (0,)), ((), ()))


def taps():
    offsets = np.arange(-RADIUS, RADIUS + 1).astype(np.float32)
    raw = np.exp(-offsets * offsets / np.float32(2.0))
    return (raw / np.sum(raw)).astype(np.float32)


def split(value):
    high = value.astype(BF16)
    return high, (value - high.astype(F32)).astype(BF16)


def dot(a, b, dims, precision=None):
    return lax.dot_general(a, b, dims, precision=precision, preferred_element_type=F32)


def band(shape, shift, weights):
    row = lax.broadcasted_iota(jnp.int32, shape, 0)
    column = lax.broadcasted_iota(jnp.int32, shape, 1)
    at = column - row - shift
    out = jnp.zeros(shape, F32)
    for a in range(-RADIUS, RADIUS + 1):
        out = jnp.where(at == a, float(weights[a + RADIUS]), out)
    return out


def block_mask(b):
    lane = lax.broadcasted_iota(jnp.int32, (8, 128), 1)
    return jnp.logical_and(lane >= 32 * b, lane < 32 * (b + 1))


def pack_gram(full):
    out = jnp.zeros((8, 128), F32)
    for b in range(4):
        out = jnp.where(block_mask(b), full[8 * b:8 * b + 8, :], out)
    return out


def unpack_gram(packed):
    return jnp.concatenate([jnp.where(block_mask(b), packed, 0.0) for b in range(4)], axis=0)


def kernel(
    spectra, loadings, profiles, out_load, out_prof,
    ext, load_in, prof_in, ysm, smooth, rows, load_flat, load_split, clean_hi, clean_lo,
    bg_all, gram_a, gram_b, prof_send, prof_1, prof_2, prof_3, prof_new,
    gram_c, part_send, part_all, new_all, pad_t,
    local_sem, halo_send, halo_recv, send_sem, recv_sem,
):
    nx = spectra.shape[0]
    ny = spectra.shape[1]
    gx, gy, ma = lax.axis_index("gx"), lax.axis_index("gy"), lax.axis_index("ma")
    count_x, count_y = lax.axis_size("gx"), lax.axis_size("gy")
    half, y = gy // GROUP, gy % GROUP
    xc = gx * 2 + half
    weights = taps()

    def z_peer(p):
        return {"gx": gx, "gy": gy, "ma": p}

    def y_peer(p):
        return {"gx": gx, "gy": half * GROUP + p, "ma": ma}

    def xc_peer(p):
        return {"gx": p // 2, "gy": (p % 2) * GROUP + y, "ma": ma}

    copy_spectra = pltpu.make_async_copy(
        spectra, ext.at[RADIUS:RADIUS + nx, SIDE:SIDE + ny, :], local_sem.at[0]
    )
    copy_load = pltpu.make_async_copy(loadings, load_in, local_sem.at[1])
    copy_prof = pltpu.make_async_copy(profiles, prof_in, local_sem.at[2])
    copy_load.start()
    copy_spectra.start()
    copy_prof.start()

    has = {
        ("x", -1): gx > 0, ("x", 0): None, ("x", 1): gx < count_x - 1,
        ("y", -1): gy > 0, ("y", 0): None, ("y", 1): gy < count_y - 1,
    }
    steps = [(0, -1), (0, 1), (-1, 0), (1, 0), (-1, -1), (-1, 1), (1, -1), (1, 1)]

    def exists(dx, dy):
        a, b = has[("x", dx)], has[("y", dy)]
        if a is None:
            return b
        if b is None:
            return a
        return jnp.logical_and(a, b)

    send_x = {-1: slice(0, RADIUS), 0: slice(0, nx), 1: slice(nx - RADIUS, nx)}
    send_y = {-1: slice(0, SIDE), 0: slice(0, ny), 1: slice(ny - SIDE, ny)}
    land_x = {-1: slice(nx + RADIUS, nx + 2 * RADIUS), 0: slice(RADIUS, RADIUS + nx), 1: slice(0, RADIUS)}
    land_y = {-1: slice(SIDE + ny, 2 * SIDE + ny), 0: slice(SIDE, SIDE + ny), 1: slice(0, SIDE)}

    def halo(i, dx, dy):
        return pltpu.make_async_remote_copy(
            src_ref=spectra.at[send_x[dx], send_y[dy], :],
            dst_ref=ext.at[land_x[dx], land_y[dy], :],
            send_sem=halo_send.at[i],
            recv_sem=halo_recv.at[i],
            device_id={"gx": gx + dx, "gy": gy + dy, "ma": ma},
            device_id_type=MESH,
        )

    barrier = pltpu.get_barrier_semaphore()
    for d in range(1, GROUP):
        for to in (z_peer((ma + d) % GROUP), y_peer((y + d) % GROUP), xc_peer((xc + d) % GROUP)):
            pl.semaphore_signal(barrier, inc=1, device_id=to, device_id_type=MESH)
    for dx, dy in steps:
        @pl.when(exists(dx, dy))
        def _():
            pl.semaphore_signal(
                barrier, inc=1, device_id={"gx": gx + dx, "gy": gy + dy, "ma": ma}, device_id_type=MESH
            )
    near_x = (gx > 0).astype(jnp.int32) + (gx < count_x - 1).astype(jnp.int32)
    near_y = (gy > 0).astype(jnp.int32) + (gy < count_y - 1).astype(jnp.int32)
    pl.semaphore_wait(barrier, 3 * (GROUP - 1) + near_x + near_y + near_x * near_y)

    for i, (dx, dy) in enumerate(steps):
        @pl.when(exists(dx, dy))
        def _():
            halo(i, dx, dy).start()

    def exchange(stage, me, peer_id, source, slots):
        for d in ORDER:
            p = (me + d) % GROUP
            send_one(stage, d, me, p, peer_id, source(p), slots)

    def send_one(stage, d, me, p, peer_id, source, slots):
        pltpu.make_async_remote_copy(
            src_ref=source,
            dst_ref=slots.at[me],
            send_sem=send_sem.at[stage, d - 1],
            recv_sem=recv_sem.at[stage, d - 1],
            device_id=peer_id(p),
            device_id_type=MESH,
        ).start()

    def arrive(stage, me, peer_id, source, slots):
        for d in ORDER[::-1]:
            p = (me + d) % GROUP
            q = (me + GROUP - d) % GROUP
            out = pltpu.make_async_remote_copy(
                src_ref=source(p),
                dst_ref=slots.at[q],
                send_sem=send_sem.at[stage, d - 1],
                recv_sem=recv_sem.at[stage, d - 1],
                device_id=peer_id(p),
                device_id_type=MESH,
            )
            out.wait_recv()
            out.wait_send()

    def total(slots):
        out = slots[0]
        for p in range(1, GROUP):
            out = out + slots[p]
        return out

    zero_x = jnp.zeros((RADIUS, ny + 2 * SIDE, ext.shape[2]), BF16)
    zero_y = jnp.zeros((nx + 2 * RADIUS, SIDE, ext.shape[2]), BF16)

    @pl.when(gx == 0)
    def _():
        ext[0:RADIUS, :, :] = zero_x

    @pl.when(gx == count_x - 1)
    def _():
        ext[nx + RADIUS:nx + 2 * RADIUS, :, :] = zero_x

    @pl.when(gy == 0)
    def _():
        ext[:, 0:SIDE, :] = zero_y

    @pl.when(gy == count_y - 1)
    def _():
        ext[:, SIDE + ny:2 * SIDE + ny, :] = zero_y

    copy_load.wait()
    for x in range(nx):
        load_flat[x // 2, :, 128 * (x % 2):128 * (x % 2) + 128] = load_in[:, x, :]
    full = jnp.zeros((32, 128), F32)
    for i in range(nx // 2):
        part = load_flat[i]
        high, low = split(part)
        load_split[i, 0:32, :] = high
        load_split[i, 32:64, :] = low
        full = full + dot(part, jnp.concatenate([part] * 4, axis=0), NT, HIGH)
    gram_a[xc] = pack_gram(full)
    exchange(0, xc, xc_peer, lambda p: gram_a.at[xc], gram_a)

    hi_taps = weights.astype(ml_dtypes.bfloat16).astype(np.float32)
    lo_taps = (weights - hi_taps).astype(ml_dtypes.bfloat16).astype(np.float32)
    wide = (ny, ny + 2 * SIDE)
    band_hi, band_lo = band(wide, SIDE, hi_taps), band(wide, SIDE, lo_taps)
    band_two = jnp.concatenate([band_hi, band_lo], axis=0).astype(BF16)
    ones = jnp.ones((8, ext.shape[2]), BF16)
    rows[...] = jnp.zeros_like(rows)

    def along_y(x):
        block = ext[x]
        both = dot(band_two, block, NN)
        ysm[x] = both[0:ny] + both[ny:2 * ny]
        rows[pl.ds(x, 1), :] = dot(ones, block, NT)[0:1, :]

    def wait_halo(i):
        dx, dy = steps[i]

        @pl.when(exists(-dx, -dy))
        def _():
            halo(i, dx, dy).wait_recv()

    wait_halo(0)
    wait_halo(1)
    copy_spectra.wait()

    @pl.loop(0, nx // 4)
    def _(i):
        for j in range(4):
            along_y(RADIUS + 4 * i + j)

    for i in range(2, 8):
        wait_halo(i)
    for x in (0, 1, nx + RADIUS, nx + RADIUS + 1):
        along_y(x)

    row_y = dot(rows[...], band_hi + band_lo, NT, HIGH)
    bg_all[ma] = dot(band((nx, rows.shape[0]), RADIUS, weights), row_y, NN, HIGH)
    exchange(1, ma, z_peer, lambda p: bg_all.at[ma], bg_all)

    arrive(0, xc, xc_peer, lambda p: gram_a.at[xc], gram_a)
    gram_b[y] = total(gram_a)
    exchange(2, y, y_peer, lambda p: gram_b.at[y], gram_b)

    w0, w1, w2 = (float(weights[RADIUS + a]) for a in range(3))

    @pl.loop(0, nx // 2)
    def _(i):
        for j in range(2):
            x = 2 * i + j
            smooth[x] = (
                w0 * ysm[x + 2] + w1 * (ysm[x + 1] + ysm[x + 3]) + w2 * (ysm[x] + ysm[x + 4])
            )

    copy_prof.wait()
    arrive(2, y, y_peer, lambda p: gram_b.at[y], gram_b)
    gram = unpack_gram(total(gram_b))
    old_prof = prof_in[...]
    below_prof = dot(gram, jnp.concatenate([old_prof] * 4, axis=0), NN, HIGH) + EPSILON

    arrive(1, ma, z_peer, lambda p: bg_all.at[ma], bg_all)
    pad_t[...] = jnp.zeros_like(pad_t)
    pad_t[0:nx, :] = total(bg_all) * (1.0 / 2048.0)
    back = pad_t[...].T

    acc = jnp.zeros((64, 256), F32)
    acc_lo = jnp.zeros((32, 256), F32)
    for i in range(nx // 2):
        for j in range(2):
            x = 2 * i + j
            value = jnp.maximum(smooth[x] - back[:, x:x + 1], 0.0)
            high, low = split(value)
            clean_hi[i, ny * j:ny * j + ny, :] = high
            clean_lo[i, ny * j:ny * j + ny, :] = low
        acc = acc + dot(load_split[i], clean_hi[i], NN)
        acc_lo = acc_lo + dot(load_split[i, 0:32, :], clean_lo[i], NN)
    numer = acc[0:32] + acc[32:64] + acc_lo

    for p in range(GROUP):
        prof_send[p] = numer[8 * (p // 2):8 * (p // 2) + 8, 128 * (p % 2):128 * (p % 2) + 128]
    exchange(3, xc, xc_peer, lambda p: prof_send.at[p], prof_1)
    prof_1[xc] = prof_send[xc]
    arrive(3, xc, xc_peer, lambda p: prof_send.at[p], prof_1)
    prof_2[y] = total(prof_1)
    exchange(4, y, y_peer, lambda p: prof_2.at[y], prof_2)
    arrive(4, y, y_peer, lambda p: prof_2.at[y], prof_2)
    prof_3[xc] = total(prof_2)
    exchange(5, xc, xc_peer, lambda p: prof_3.at[xc], prof_3)
    arrive(5, xc, xc_peer, lambda p: prof_3.at[xc], prof_3)
    numer_prof = jnp.concatenate(
        [jnp.concatenate([prof_3[2 * b], prof_3[2 * b + 1]], axis=1) for b in range(4)], axis=0
    )
    new_prof = old_prof * numer_prof / below_prof
    prof_new[...] = new_prof
    copy_new = pltpu.make_async_copy(prof_new, out_prof, local_sem.at[3])
    copy_new.start()

    prof_hi, prof_lo = split(new_prof)
    prof_two = jnp.concatenate([prof_hi, prof_lo], axis=0)

    def loading_part(p):
        both = dot(prof_two, clean_hi[p], NT)
        return both[0:32] + both[32:64] + dot(prof_hi, clean_lo[p], NT)

    for d in ORDER:
        p = (ma + d) % GROUP
        part_send[p] = loading_part(p)
        send_one(6, d, ma, p, z_peer, part_send.at[p], part_all)
    gram_c[ma] = pack_gram(dot(new_prof, jnp.concatenate([new_prof] * 4, axis=0), NT, HIGH))
    exchange(7, ma, z_peer, lambda p: gram_c.at[ma], gram_c)
    part_all[ma] = loading_part(ma)

    arrive(7, ma, z_peer, lambda p: gram_c.at[ma], gram_c)
    mine = load_flat[ma]
    below = dot(unpack_gram(total(gram_c)), jnp.concatenate([mine] * 4, axis=0), NN, HIGH) + EPSILON
    arrive(6, ma, z_peer, lambda p: part_send.at[p], part_all)
    new_all[...] = mine * total(part_all) / below

    for d in ORDER:
        p = (ma + d) % GROUP
        send_one(8, d, ma, p, z_peer, new_all, out_load)
    copy_mine = pltpu.make_async_copy(new_all, out_load.at[ma], local_sem.at[4])
    copy_mine.start()
    for i, (dx, dy) in enumerate(steps):
        @pl.when(exists(dx, dy))
        def _():
            halo(i, dx, dy).wait_send()
    copy_new.wait()
    copy_mine.wait()
    arrive(8, ma, z_peer, lambda p: new_all, out_load)


def per_device(spectra, loadings, profiles):
    nx, ny, nm = spectra.shape
    nk = loadings.shape[0]
    wide_x, wide_y = nx + 2 * RADIUS, ny + 2 * SIDE
    anywhere = pl.BlockSpec(memory_space=pl.ANY)
    vmem = pltpu.VMEM
    pieces, new_prof = pl.pallas_call(
        kernel,
        out_shape=(
            jax.ShapeDtypeStruct((GROUP, nk, 2 * ny), F32),
            jax.ShapeDtypeStruct((nk, nm), F32),
        ),
        in_specs=[anywhere] * 3,
        out_specs=(anywhere, anywhere),
        scratch_shapes=[
            vmem((wide_x, wide_y, nm), BF16),
            vmem((nk, nx, ny), F32),
            vmem((nk, nm), F32),
            vmem((wide_x, ny, nm), F32),
            vmem((nx, ny, nm), F32),
            vmem((24, wide_y), F32),
            vmem((GROUP, nk, 2 * ny), F32),
            vmem((GROUP, 2 * nk, 2 * ny), BF16),
            vmem((GROUP, 2 * ny, nm), BF16),
            vmem((GROUP, 2 * ny, nm), BF16),
            vmem((GROUP, nx, ny), F32),
            vmem((GROUP, 8, 128), F32),
            vmem((GROUP, 8, 128), F32),
            vmem((GROUP, 8, 128), F32),
            vmem((GROUP, 8, 128), F32),
            vmem((GROUP, 8, 128), F32),
            vmem((GROUP, 8, 128), F32),
            vmem((nk, nm), F32),
            vmem((GROUP, 8, 128), F32),
            vmem((GROUP, nk, 2 * ny), F32),
            vmem((GROUP, nk, 2 * ny), F32),
            vmem((nk, 2 * ny), F32),
            vmem((128, 128), F32),
            pltpu.SemaphoreType.DMA((5,)),
            pltpu.SemaphoreType.DMA((8,)),
            pltpu.SemaphoreType.DMA((8,)),
            pltpu.SemaphoreType.DMA((9, GROUP - 1)),
            pltpu.SemaphoreType.DMA((9, GROUP - 1)),
        ],
        compiler_params=pltpu.CompilerParams(
            collective_id=0, has_side_effects=True, vmem_limit_bytes=40 * 1024 * 1024
        ),
    )(spectra, loadings, profiles)
    new_load = jnp.transpose(pieces.reshape(GROUP, nk, 2, ny), (1, 0, 2, 3)).reshape(nk, nx, ny)
    return new_load, new_prof


def solution(mesh):
    return jax.shard_map(
        per_device,
        mesh=mesh,
        in_specs=(P("gx", "gy", "ma"), P(None, "gx", "gy"), P(None, "ma")),
        out_specs=(P(None, "gx", "gy"), P(None, "ma")),
        check_vma=False,
    )
```

```python
import jax
import jax.numpy as jnp
import ml_dtypes
import numpy as np
from jax import lax
from jax.experimental import pallas as pl
from jax.experimental.pallas import tpu as pltpu
from jax.sharding import PartitionSpec as P

MESH = pl.DeviceIdType.MESH
F32 = jnp.float32
BF16 = jnp.bfloat16
HIGH = lax.Precision.HIGHEST

RADIUS = 2
SIDE = 16
GROUP = 8
EPSILON = 1e-06
ORDER = (4, 3, 5, 2, 6, 1, 7)

NT = (((1,), (1,)), ((), ()))
NN = (((1,), (0,)), ((), ()))


def taps():
    offsets = np.arange(-RADIUS, RADIUS + 1).astype(np.float32)
    raw = np.exp(-offsets * offsets / np.float32(2.0))
    return (raw / np.sum(raw)).astype(np.float32)


def split(value):
    high = value.astype(BF16)
    return high, (value - high.astype(F32)).astype(BF16)


def dot(a, b, dims, precision=None):
    return lax.dot_general(a, b, dims, precision=precision, preferred_element_type=F32)


def band(shape, shift, weights):
    row = lax.broadcasted_iota(jnp.int32, shape, 0)
    column = lax.broadcasted_iota(jnp.int32, shape, 1)
    at = column - row - shift
    out = jnp.zeros(shape, F32)
    for a in range(-RADIUS, RADIUS + 1):
        out = jnp.where(at == a, float(weights[a + RADIUS]), out)
    return out


def block_mask(b):
    lane = lax.broadcasted_iota(jnp.int32, (8, 128), 1)
    return jnp.logical_and(lane >= 32 * b, lane < 32 * (b + 1))


def pack_gram(full):
    out = jnp.zeros((8, 128), F32)
    for b in range(4):
        out = jnp.where(block_mask(b), full[8 * b:8 * b + 8, :], out)
    return out


def unpack_gram(packed):
    return jnp.concatenate([jnp.where(block_mask(b), packed, 0.0) for b in range(4)], axis=0)


def kernel(
    spectra, loadings, profiles, out_load, out_prof,
    ext, load_in, prof_in, ysm, smooth, rows, load_flat, load_split, clean_hi, clean_lo,
    bg_all, gram_a, gram_b, prof_send, prof_1, prof_2, prof_3, prof_new,
    gram_c, part_send, part_all, below_all, new_all, pad_t,
    local_sem, halo_send, halo_recv, send_sem, recv_sem, part_recv,
):
    nx, ny, nm = spectra.shape
    nk = loadings.shape[0]
    own = nk // GROUP
    gx, gy, ma = lax.axis_index("gx"), lax.axis_index("gy"), lax.axis_index("ma")
    count_x, count_y = lax.axis_size("gx"), lax.axis_size("gy")
    half, y = gy // GROUP, gy % GROUP
    xc = gx * 2 + half
    weights = taps()

    def z_peer(p):
        return {"gx": gx, "gy": gy, "ma": p}

    def y_peer(p):
        return {"gx": gx, "gy": half * GROUP + p, "ma": ma}

    def xc_peer(p):
        return {"gx": p // 2, "gy": (p % 2) * GROUP + y, "ma": ma}

    copy_spectra = pltpu.make_async_copy(
        spectra, ext.at[RADIUS:RADIUS + nx, SIDE:SIDE + ny, :], local_sem.at[0]
    )
    copy_load = pltpu.make_async_copy(loadings, load_in, local_sem.at[1])
    copy_prof = pltpu.make_async_copy(profiles, prof_in, local_sem.at[2])

    has = {
        ("x", -1): gx > 0, ("x", 0): None, ("x", 1): gx < count_x - 1,
        ("y", -1): gy > 0, ("y", 0): None, ("y", 1): gy < count_y - 1,
    }
    steps = [(-1, 0), (1, 0), (0, -1), (0, 1), (-1, -1), (-1, 1), (1, -1), (1, 1)]

    def exists(dx, dy):
        a, b = has[("x", dx)], has[("y", dy)]
        if a is None:
            return b
        if b is None:
            return a
        return jnp.logical_and(a, b)

    send_x = {-1: slice(0, RADIUS), 0: slice(0, nx), 1: slice(nx - RADIUS, nx)}
    send_y = {-1: slice(0, SIDE), 0: slice(0, ny), 1: slice(ny - SIDE, ny)}
    land_x = {-1: slice(nx + RADIUS, nx + 2 * RADIUS), 0: slice(RADIUS, RADIUS + nx), 1: slice(0, RADIUS)}
    land_y = {-1: slice(SIDE + ny, 2 * SIDE + ny), 0: slice(SIDE, SIDE + ny), 1: slice(0, SIDE)}

    def halo(i, dx, dy):
        return pltpu.make_async_remote_copy(
            src_ref=spectra.at[send_x[dx], send_y[dy], :],
            dst_ref=ext.at[land_x[dx], land_y[dy], :],
            send_sem=halo_send.at[i],
            recv_sem=halo_recv.at[i],
            device_id={"gx": gx + dx, "gy": gy + dy, "ma": ma},
            device_id_type=MESH,
        )

    barrier = pltpu.get_barrier_semaphore()
    for dx, dy in steps:
        @pl.when(exists(dx, dy))
        def _():
            pl.semaphore_signal(
                barrier, inc=1, device_id={"gx": gx + dx, "gy": gy + dy, "ma": ma}, device_id_type=MESH
            )
    for d in ORDER:
        for to in (z_peer((ma + d) % GROUP), y_peer((y + d) % GROUP), xc_peer((xc + d) % GROUP)):
            pl.semaphore_signal(barrier, inc=1, device_id=to, device_id_type=MESH)
    copy_spectra.start()
    copy_load.start()
    copy_prof.start()
    near_x = (gx > 0).astype(jnp.int32) + (gx < count_x - 1).astype(jnp.int32)
    near_y = (gy > 0).astype(jnp.int32) + (gy < count_y - 1).astype(jnp.int32)
    pl.semaphore_wait(barrier, 3 * (GROUP - 1) + near_x + near_y + near_x * near_y)

    for i, (dx, dy) in enumerate(steps):
        @pl.when(exists(dx, dy))
        def _():
            halo(i, dx, dy).start()

    def copy(stage, source, target, device, recv=None):
        return pltpu.make_async_remote_copy(
            src_ref=source,
            dst_ref=target,
            send_sem=send_sem.at[stage],
            recv_sem=recv_sem.at[stage] if recv is None else recv,
            device_id=device,
            device_id_type=MESH,
        )

    def exchange(stage, me, peer_id, source, slots):
        for d in ORDER:
            p = (me + d) % GROUP
            copy(stage, source(p), slots.at[me], peer_id(p)).start()

    def arrive(stage, me, peer_id, slots):
        whole = slots.at[0:GROUP - 1]
        copy(stage, whole, whole, peer_id((me + 1) % GROUP)).wait_recv()

    def sent(stage, me, peer_id, slots):
        whole = slots.at[0:GROUP - 1]
        copy(stage, whole, whole, peer_id((me + 1) % GROUP)).wait_send()

    def total(slots):
        out = slots[0]
        for p in range(1, GROUP):
            out = out + slots[p]
        return out

    zero_x = jnp.zeros((RADIUS, ny + 2 * SIDE, nm), BF16)
    zero_y = jnp.zeros((nx + 2 * RADIUS, SIDE, nm), BF16)

    @pl.when(gx == 0)
    def _():
        ext[0:RADIUS, :, :] = zero_x

    @pl.when(gx == count_x - 1)
    def _():
        ext[nx + RADIUS:nx + 2 * RADIUS, :, :] = zero_x

    @pl.when(gy == 0)
    def _():
        ext[:, 0:SIDE, :] = zero_y

    @pl.when(gy == count_y - 1)
    def _():
        ext[:, SIDE + ny:2 * SIDE + ny, :] = zero_y

    copy_load.wait()
    for x in range(nx):
        load_flat[x // 2, :, 128 * (x % 2):128 * (x % 2) + 128] = load_in[:, x, :]
    full = jnp.zeros((32, 128), F32)
    for i in range(nx // 2):
        part = load_flat[i]
        high, low = split(part)
        load_split[i, 0:32, :] = high
        load_split[i, 32:64, :] = low
        full = full + dot(part, jnp.concatenate([part] * 4, axis=0), NT, HIGH)
    gram_a[xc] = pack_gram(full)
    exchange(0, xc, xc_peer, lambda p: gram_a.at[xc], gram_a)

    ones = jnp.ones((8, nm), BF16)
    rows[...] = jnp.zeros_like(rows)

    def sum_bins(x):
        rows[x:x + 1, :] = dot(ones, ext[x], NT)[0:1, :]

    def wait_halo(i):
        dx, dy = steps[i]

        @pl.when(exists(-dx, -dy))
        def _():
            halo(i, dx, dy).wait_recv()

    copy_spectra.wait()
    wait_halo(2)
    wait_halo(3)
    for x in range(RADIUS, nx + RADIUS):
        sum_bins(x)
    for i in (0, 1, 4, 5, 6, 7):
        wait_halo(i)
    for x in (0, 1, nx + RADIUS, nx + RADIUS + 1):
        sum_bins(x)

    hi_taps = weights.astype(ml_dtypes.bfloat16).astype(np.float32)
    lo_taps = (weights - hi_taps).astype(ml_dtypes.bfloat16).astype(np.float32)
    wide = (ny, ny + 2 * SIDE)
    band_hi, band_lo = band(wide, SIDE, hi_taps), band(wide, SIDE, lo_taps)
    w0, w1, w2 = (float(weights[RADIUS + a]) for a in range(3))
    row_x = (
        w0 * rows[2:nx + 2, :] + w1 * (rows[1:nx + 1, :] + rows[3:nx + 3, :])
        + w2 * (rows[0:nx, :] + rows[4:nx + 4, :])
    )
    bg_all[ma] = dot(row_x, band_hi + band_lo, NT, HIGH)
    exchange(1, ma, z_peer, lambda p: bg_all.at[ma], bg_all)

    arrive(0, xc, xc_peer, gram_a)
    gram_b[y] = total(gram_a)
    exchange(2, y, y_peer, lambda p: gram_b.at[y], gram_b)
    band_two = jnp.concatenate([band_hi, band_lo], axis=0).astype(BF16)

    @pl.loop(0, (nx + 2 * RADIUS) // 4)
    def _(i):
        for j in range(4):
            x = 4 * i + j
            both = dot(band_two, ext[x], NN)
            ysm[x] = both[0:ny] + both[ny:2 * ny]

    @pl.loop(0, nx // 2)
    def _(i):
        for j in range(2):
            x = 2 * i + j
            smooth[x] = (
                w0 * ysm[x + 2] + w1 * (ysm[x + 1] + ysm[x + 3]) + w2 * (ysm[x] + ysm[x + 4])
            )

    copy_prof.wait()
    arrive(2, y, y_peer, gram_b)
    gram = unpack_gram(total(gram_b))
    old_prof = prof_in[...]
    below_prof = dot(gram, jnp.concatenate([old_prof] * 4, axis=0), NN, HIGH) + EPSILON

    arrive(1, ma, z_peer, bg_all)
    pad_t[0:nx, :] = total(bg_all) * (1.0 / 2048.0)
    back = pad_t[...].T

    acc = jnp.zeros((64, 256), F32)
    acc_lo = jnp.zeros((32, 256), F32)
    for i in range(nx // 2):
        for j in range(2):
            x = 2 * i + j
            value = jnp.maximum(smooth[x] - back[:, x:x + 1], 0.0)
            high, low = split(value)
            clean_hi[i, ny * j:ny * j + ny, :] = high
            clean_lo[i, ny * j:ny * j + ny, :] = low
        acc = acc + dot(load_split[i], clean_hi[i], NN)
        acc_lo = acc_lo + dot(load_split[i, 0:32, :], clean_lo[i], NN)
    numer = acc[0:32] + acc[32:64] + acc_lo

    for p in range(GROUP):
        prof_send[p] = numer[8 * (p // 2):8 * (p // 2) + 8, 128 * (p % 2):128 * (p % 2) + 128]
    exchange(3, xc, xc_peer, lambda p: prof_send.at[p], prof_1)
    prof_1[xc] = prof_send[xc]
    arrive(3, xc, xc_peer, prof_1)
    prof_2[y] = total(prof_1)
    exchange(4, y, y_peer, lambda p: prof_2.at[y], prof_2)
    arrive(4, y, y_peer, prof_2)
    prof_3[xc] = total(prof_2)
    exchange(5, xc, xc_peer, lambda p: prof_3.at[xc], prof_3)
    arrive(5, xc, xc_peer, prof_3)
    numer_prof = jnp.concatenate(
        [jnp.concatenate([prof_3[2 * b], prof_3[2 * b + 1]], axis=1) for b in range(4)], axis=0
    )
    new_prof = old_prof * numer_prof / below_prof

    prof_hi, prof_lo = split(new_prof)
    prof_two = jnp.concatenate([prof_hi, prof_lo], axis=0)
    for i in range(nx // 2):
        both = dot(prof_two, clean_hi[i], NT)
        part = both[0:32] + both[32:64] + dot(prof_hi, clean_lo[i], NT)
        part_send[:, 2 * i, :] = part[:, 0:ny]
        part_send[:, 2 * i + 1, :] = part[:, ny:2 * ny]
    for c in range(own):
        for d in ORDER:
            p = (ma + d) % GROUP
            copy(6, part_send.at[own * p + c], part_all.at[c, d - 1], z_peer(p), part_recv.at[c]).start()
        if c == 0:
            gram_c[ma] = pack_gram(dot(new_prof, jnp.concatenate([new_prof] * 4, axis=0), NT, HIGH))
            exchange(7, ma, z_peer, lambda p: gram_c.at[ma], gram_c)
    prof_new[...] = new_prof
    copy_new = pltpu.make_async_copy(prof_new, out_prof, local_sem.at[3])
    copy_new.start()

    arrive(7, ma, z_peer, gram_c)
    lane = lax.broadcasted_iota(jnp.int32, (8, 128), 1)
    block = ma // 2
    mask = jnp.logical_and(lane >= 32 * block, lane < 32 * block + 32)
    gram_rows = jnp.where(mask, total(gram_c), 0.0)
    for i in range(nx // 2):
        below = dot(gram_rows, jnp.concatenate([load_flat[i]] * 4, axis=0), NN, HIGH) + EPSILON
        below_all[:, 2 * i, :] = below[:, 0:ny]
        below_all[:, 2 * i + 1, :] = below[:, ny:2 * ny]

    for c in range(own):
        whole = part_all.at[c]
        copy(6, whole, whole, z_peer((ma + 1) % GROUP), part_recv.at[c]).wait_recv()
        k = own * ma + c
        value = part_send[k]
        for d in range(GROUP - 1):
            value = value + part_all[c, d]
        new_all[c] = load_in[k] * value / below_all[own * (ma % 2) + c]
        for p in range(GROUP):
            @pl.when(ma != p)
            def _():
                copy(8, new_all.at[c], out_load.at[k], z_peer(p)).start()
    copy_mine = pltpu.make_async_copy(new_all, out_load.at[pl.ds(own * ma, own)], local_sem.at[4])
    copy_mine.start()

    for i, (dx, dy) in enumerate(steps):
        @pl.when(exists(dx, dy))
        def _():
            halo(i, dx, dy).wait_send()
    sent(0, xc, xc_peer, gram_a)
    sent(1, ma, z_peer, bg_all)
    sent(2, y, y_peer, gram_b)
    sent(3, xc, xc_peer, prof_1)
    sent(4, y, y_peer, prof_2)
    sent(5, xc, xc_peer, prof_3)
    sent(7, ma, z_peer, gram_c)
    peer = z_peer((ma + 1) % GROUP)
    copy(6, part_all, part_all, peer).wait_send()
    copy_new.wait()
    copy_mine.wait()
    most = out_load.at[0:nk - own]
    copy(8, most, most, peer).wait_send()
    copy(8, most, most, peer).wait_recv()


def per_device(spectra, loadings, profiles):
    nx, ny, nm = spectra.shape
    nk = loadings.shape[0]
    own = nk // GROUP
    wide_x, wide_y = nx + 2 * RADIUS, ny + 2 * SIDE
    anywhere = pl.BlockSpec(memory_space=pl.ANY)
    vmem = pltpu.VMEM
    return pl.pallas_call(
        kernel,
        out_shape=(
            jax.ShapeDtypeStruct((nk, nx, ny), F32),
            jax.ShapeDtypeStruct((nk, nm), F32),
        ),
        in_specs=[anywhere] * 3,
        out_specs=(anywhere, anywhere),
        scratch_shapes=[
            vmem((wide_x, wide_y, nm), BF16),
            vmem((nk, nx, ny), F32),
            vmem((nk, nm), F32),
            vmem((wide_x, ny, nm), F32),
            vmem((nx, ny, nm), F32),
            vmem((24, wide_y), F32),
            vmem((nx // 2, nk, 2 * ny), F32),
            vmem((nx // 2, 2 * nk, 2 * ny), BF16),
            vmem((nx // 2, 2 * ny, nm), BF16),
            vmem((nx // 2, 2 * ny, nm), BF16),
            vmem((GROUP, nx, ny), F32),
            vmem((GROUP, 8, 128), F32),
            vmem((GROUP, 8, 128), F32),
            vmem((GROUP, 8, 128), F32),
            vmem((GROUP, 8, 128), F32),
            vmem((GROUP, 8, 128), F32),
            vmem((GROUP, 8, 128), F32),
            vmem((nk, nm), F32),
            vmem((GROUP, 8, 128), F32),
            vmem((nk, nx, ny), F32),
            vmem((own, GROUP - 1, nx, ny), F32),
            vmem((8, nx, ny), F32),
            vmem((own, nx, ny), F32),
            vmem((128, 128), F32),
            pltpu.SemaphoreType.DMA((5,)),
            pltpu.SemaphoreType.DMA((8,)),
            pltpu.SemaphoreType.DMA((8,)),
            pltpu.SemaphoreType.DMA((9,)),
            pltpu.SemaphoreType.DMA((9,)),
            pltpu.SemaphoreType.DMA((own,)),
        ],
        compiler_params=pltpu.CompilerParams(
            collective_id=0, has_side_effects=True, vmem_limit_bytes=60 * 1024 * 1024
        ),
    )(spectra, loadings, profiles)


def solution(mesh):
    return jax.shard_map(
        per_device,
        mesh=mesh,
        in_specs=(P("gx", "gy", "ma"), P(None, "gx", "gy"), P(None, "ma")),
        out_specs=(P(None, "gx", "gy"), P(None, "ma")),
        check_vma=False,
    )
```

```python
import jax
import jax.numpy as jnp
import ml_dtypes
import numpy as np
from jax import lax
from jax.experimental import pallas as pl
from jax.experimental.pallas import tpu as pltpu
from jax.sharding import PartitionSpec as P

MESH = pl.DeviceIdType.MESH
F32 = jnp.float32
BF16 = jnp.bfloat16
HIGH = lax.Precision.HIGHEST

RADIUS = 2
SIDE = 16
GROUP = 8
EPSILON = 1e-06
ORDER = (4, 3, 5, 2, 6, 1, 7)

NT = (((1,), (1,)), ((), ()))
NN = (((1,), (0,)), ((), ()))


def taps():
    offsets = np.arange(-RADIUS, RADIUS + 1).astype(np.float32)
    raw = np.exp(-offsets * offsets / np.float32(2.0))
    return (raw / np.sum(raw)).astype(np.float32)


def split(value):
    high = value.astype(BF16)
    return high, (value - high.astype(F32)).astype(BF16)


def dot(a, b, dims, precision=None):
    return lax.dot_general(a, b, dims, precision=precision, preferred_element_type=F32)


def band(shape, shift, weights):
    row = lax.broadcasted_iota(jnp.int32, shape, 0)
    column = lax.broadcasted_iota(jnp.int32, shape, 1)
    at = column - row - shift
    out = jnp.zeros(shape, F32)
    for a in range(-RADIUS, RADIUS + 1):
        out = jnp.where(at == a, float(weights[a + RADIUS]), out)
    return out


def block_mask(b):
    lane = lax.broadcasted_iota(jnp.int32, (8, 128), 1)
    return jnp.logical_and(lane >= 32 * b, lane < 32 * (b + 1))


def pack_gram(full):
    out = jnp.zeros((8, 128), F32)
    for b in range(4):
        out = jnp.where(block_mask(b), full[8 * b:8 * b + 8, :], out)
    return out


def unpack_gram(packed):
    return jnp.concatenate([jnp.where(block_mask(b), packed, 0.0) for b in range(4)], axis=0)


def kernel(
    spectra, loadings, profiles, out_load, out_prof,
    ext, load_in, prof_in, ysm, smooth, rows, load_flat, load_split, clean_hi, clean_lo,
    bg_all, gram_a, gram_b, prof_send, prof_1, prof_2, prof_3, prof_new,
    gram_c, part_send, part_all, below_all, new_all, pad_t,
    sums_own, sums_in, edge_own, edge_in, local_sem, sums_send, sums_recv, halo_send, halo_recv, send_sem, recv_sem, part_recv,
):
    nx, ny, nm = spectra.shape
    nk = loadings.shape[0]
    own = nk // GROUP
    gx, gy, ma = lax.axis_index("gx"), lax.axis_index("gy"), lax.axis_index("ma")
    count_x, count_y = lax.axis_size("gx"), lax.axis_size("gy")
    half, y = gy // GROUP, gy % GROUP
    xc = gx * 2 + half
    weights = taps()

    def z_peer(p):
        return {"gx": gx, "gy": gy, "ma": p}

    def y_peer(p):
        return {"gx": gx, "gy": half * GROUP + p, "ma": ma}

    def xc_peer(p):
        return {"gx": p // 2, "gy": (p % 2) * GROUP + y, "ma": ma}

    copy_spectra = pltpu.make_async_copy(
        spectra, ext.at[RADIUS:RADIUS + nx, SIDE:SIDE + ny, :], local_sem.at[0]
    )
    copy_load = pltpu.make_async_copy(loadings, load_in, local_sem.at[1])
    copy_prof = pltpu.make_async_copy(profiles, prof_in, local_sem.at[2])

    has = {
        ("x", -1): gx > 0, ("x", 0): None, ("x", 1): gx < count_x - 1,
        ("y", -1): gy > 0, ("y", 0): None, ("y", 1): gy < count_y - 1,
    }
    steps = [(-1, 0), (1, 0), (0, -1), (0, 1), (-1, -1), (-1, 1), (1, -1), (1, 1)]

    def exists(dx, dy):
        a, b = has[("x", dx)], has[("y", dy)]
        if a is None:
            return b
        if b is None:
            return a
        return jnp.logical_and(a, b)

    rows_out = {-1: slice(0, 16), 0: slice(0, 2 * nx), 1: slice(2 * nx - 16, 2 * nx)}
    rows_land = {-1: slice(16 + 2 * nx, 32 + 2 * nx), 0: slice(16, 16 + 2 * nx), 1: slice(0, 16)}
    middle = slice(SIDE, SIDE + ny)

    def halo_refs(dx, dy):
        if dy == 0:
            first, land = (RADIUS, nx + RADIUS) if dx < 0 else (nx, 0)
            return ext.at[first:first + RADIUS, middle, :], ext.at[land:land + RADIUS, middle, :]
        side = (dy + 1) // 2
        return edge_own.at[side, rows_out[dx], :], edge_in.at[1 - side, rows_land[dx], :]

    def halo(i, dx, dy):
        source, target = halo_refs(dx, dy)
        return pltpu.make_async_remote_copy(
            src_ref=source,
            dst_ref=target,
            send_sem=halo_send.at[i],
            recv_sem=halo_recv.at[i],
            device_id={"gx": gx + dx, "gy": gy + dy, "ma": ma},
            device_id_type=MESH,
        )

    barrier = pltpu.get_barrier_semaphore()
    for dx, dy in steps:
        @pl.when(exists(dx, dy))
        def _():
            pl.semaphore_signal(
                barrier, inc=1, device_id={"gx": gx + dx, "gy": gy + dy, "ma": ma}, device_id_type=MESH
            )
    for d in ORDER:
        for to in (z_peer((ma + d) % GROUP), y_peer((y + d) % GROUP), xc_peer((xc + d) % GROUP)):
            pl.semaphore_signal(barrier, inc=1, device_id=to, device_id_type=MESH)
    copy_spectra.start()
    copy_load.start()
    copy_prof.start()

    copy_spectra.wait()
    ones = jnp.ones((8, nm), BF16)
    for x in range(nx):
        sums_own[x:x + 1, :] = dot(ones, ext[RADIUS + x, SIDE:SIDE + ny, :], NT)[0:1, :]
    at = lax.broadcasted_iota(jnp.int32, (2 * nx, 16 * nx), 0)
    column = lax.broadcasted_iota(jnp.int32, (2 * nx, 16 * nx), 1)
    for side, first in ((0, SIDE), (1, SIDE + ny - 16)):
        tile = ext[RADIUS:RADIUS + nx, first:first + 16, :].reshape(16 * nx, nm)
        pick = column == 16 * (at >> 1) + (at & 1) + side * (16 - RADIUS)
        edge_own[side] = dot(jnp.where(pick, 1.0, 0.0).astype(BF16), tile, NN).astype(BF16)

    near_x = (gx > 0).astype(jnp.int32) + (gx < count_x - 1).astype(jnp.int32)
    near_y = (gy > 0).astype(jnp.int32) + (gy < count_y - 1).astype(jnp.int32)
    pl.semaphore_wait(barrier, 3 * (GROUP - 1) + near_x + near_y + near_x * near_y)

    def sums(i, dx, dy):
        return pltpu.make_async_remote_copy(
            src_ref=sums_own,
            dst_ref=sums_in.at[i],
            send_sem=sums_send.at[i],
            recv_sem=sums_recv.at[i],
            device_id={"gx": gx + dx, "gy": gy + dy, "ma": ma},
            device_id_type=MESH,
        )

    for make in (sums, halo):
        for i, (dx, dy) in enumerate(steps):
            @pl.when(exists(dx, dy))
            def _():
                make(i, dx, dy).start()

    def copy(stage, source, target, device, recv=None):
        return pltpu.make_async_remote_copy(
            src_ref=source,
            dst_ref=target,
            send_sem=send_sem.at[stage],
            recv_sem=recv_sem.at[stage] if recv is None else recv,
            device_id=device,
            device_id_type=MESH,
        )

    def exchange(stage, me, peer_id, source, slots):
        for d in ORDER:
            p = (me + d) % GROUP
            copy(stage, source(p), slots.at[me], peer_id(p)).start()

    def arrive(stage, me, peer_id, slots):
        whole = slots.at[0:GROUP - 1]
        copy(stage, whole, whole, peer_id((me + 1) % GROUP)).wait_recv()

    def sent(stage, me, peer_id, slots):
        whole = slots.at[0:GROUP - 1]
        copy(stage, whole, whole, peer_id((me + 1) % GROUP)).wait_send()

    def total(slots):
        out = slots[0]
        for p in range(1, GROUP):
            out = out + slots[p]
        return out

    for dx, dy in steps:
        @pl.when(jnp.logical_not(exists(-dx, -dy)))
        def _():
            unused, target = halo_refs(dx, dy)
            target[...] = jnp.zeros(target.shape, BF16)

    copy_load.wait()
    for x in range(nx):
        load_flat[x // 2, :, 128 * (x % 2):128 * (x % 2) + 128] = load_in[:, x, :]
    full = jnp.zeros((32, 128), F32)
    for i in range(nx // 2):
        part = load_flat[i]
        high, low = split(part)
        load_split[i, 0:32, :] = high
        load_split[i, 32:64, :] = low
        full = full + dot(part, jnp.concatenate([part] * 4, axis=0), NT, HIGH)
    gram_a[xc] = pack_gram(full)
    exchange(0, xc, xc_peer, lambda p: gram_a.at[xc], gram_a)

    for i, (dx, dy) in enumerate(steps):
        there = exists(-dx, -dy)

        @pl.when(there)
        def _():
            sums(i, dx, dy).wait_recv()

        @pl.when(jnp.logical_not(there))
        def _():
            sums_in[i] = jnp.zeros_like(sums_own)
    for side in (-1, 0, 1):
        columns = slice(ny * (side + 1), ny * (side + 2))
        low, high = steps.index((1, -side)), steps.index((-1, -side))
        rows[0:RADIUS, columns] = sums_in[low, nx - RADIUS:nx, :]
        rows[RADIUS:nx + RADIUS, columns] = sums_own[...] if side == 0 else sums_in[steps.index((0, -side))]
        rows[nx + RADIUS:nx + 2 * RADIUS, columns] = sums_in[high, 0:RADIUS, :]

    hi_taps = weights.astype(ml_dtypes.bfloat16).astype(np.float32)
    lo_taps = (weights - hi_taps).astype(ml_dtypes.bfloat16).astype(np.float32)
    wide = (ny, ny + 2 * SIDE)
    both_taps = hi_taps + lo_taps
    w0, w1, w2 = (float(weights[RADIUS + a]) for a in range(3))
    row_x = (
        w0 * rows[2:nx + 2, :] + w1 * (rows[1:nx + 1, :] + rows[3:nx + 3, :])
        + w2 * (rows[0:nx, :] + rows[4:nx + 4, :])
    )
    bg_all[ma] = dot(row_x, band((ny, 3 * ny), ny, both_taps), NT, HIGH)
    exchange(1, ma, z_peer, lambda p: bg_all.at[ma], bg_all)

    arrive(0, xc, xc_peer, gram_a)
    gram_b[y] = total(gram_a)
    exchange(2, y, y_peer, lambda p: gram_b.at[y], gram_b)
    band_two = jnp.concatenate(
        [band(wide, SIDE, hi_taps), band(wide, SIDE, lo_taps)], axis=0
    ).astype(BF16)
    for i, (dx, dy) in enumerate(steps):
        @pl.when(exists(-dx, -dy))
        def _():
            halo(i, dx, dy).wait_recv()
    at = lax.broadcasted_iota(jnp.int32, (16 * (nx + 2 * RADIUS), edge_in.shape[1]), 0)
    column = lax.broadcasted_iota(jnp.int32, (16 * (nx + 2 * RADIUS), edge_in.shape[1]), 1)
    for side, first in ((0, SIDE - 16), (1, SIDE + ny)):
        inside = (at & 15) - (16 - RADIUS) * (1 - side)
        pick = jnp.logical_and(
            column == 12 + 2 * (at >> 4) + inside, jnp.logical_and(inside >= 0, inside < RADIUS)
        )
        spread = dot(jnp.where(pick, 1.0, 0.0).astype(BF16), edge_in[side], NN).astype(BF16)
        ext[:, first:first + 16, :] = spread.reshape(nx + 2 * RADIUS, 16, nm)

    @pl.loop(0, (nx + 2 * RADIUS) // 4)
    def _(i):
        for j in range(4):
            x = 4 * i + j
            both = dot(band_two, ext[x], NN)
            ysm[x] = both[0:ny] + both[ny:2 * ny]

    @pl.loop(0, nx // 2)
    def _(i):
        for j in range(2):
            x = 2 * i + j
            smooth[x] = (
                w0 * ysm[x + 2] + w1 * (ysm[x + 1] + ysm[x + 3]) + w2 * (ysm[x] + ysm[x + 4])
            )

    copy_prof.wait()
    arrive(2, y, y_peer, gram_b)
    gram = unpack_gram(total(gram_b))
    old_prof = prof_in[...]
    below_prof = dot(gram, jnp.concatenate([old_prof] * 4, axis=0), NN, HIGH) + EPSILON

    arrive(1, ma, z_peer, bg_all)
    pad_t[0:nx, :] = total(bg_all) * (1.0 / 2048.0)
    back = pad_t[...].T

    acc = jnp.zeros((64, 256), F32)
    acc_lo = jnp.zeros((32, 256), F32)
    for i in range(nx // 2):
        for j in range(2):
            x = 2 * i + j
            value = jnp.maximum(smooth[x] - back[:, x:x + 1], 0.0)
            high, low = split(value)
            clean_hi[i, ny * j:ny * j + ny, :] = high
            clean_lo[i, ny * j:ny * j + ny, :] = low
        acc = acc + dot(load_split[i], clean_hi[i], NN)
        acc_lo = acc_lo + dot(load_split[i, 0:32, :], clean_lo[i], NN)
    numer = acc[0:32] + acc[32:64] + acc_lo

    for p in range(GROUP):
        prof_send[p] = numer[8 * (p // 2):8 * (p // 2) + 8, 128 * (p % 2):128 * (p % 2) + 128]
    exchange(3, xc, xc_peer, lambda p: prof_send.at[p], prof_1)
    prof_1[xc] = prof_send[xc]
    arrive(3, xc, xc_peer, prof_1)
    prof_2[y] = total(prof_1)
    exchange(4, y, y_peer, lambda p: prof_2.at[y], prof_2)
    arrive(4, y, y_peer, prof_2)
    prof_3[xc] = total(prof_2)
    exchange(5, xc, xc_peer, lambda p: prof_3.at[xc], prof_3)
    arrive(5, xc, xc_peer, prof_3)
    numer_prof = jnp.concatenate(
        [jnp.concatenate([prof_3[2 * b], prof_3[2 * b + 1]], axis=1) for b in range(4)], axis=0
    )
    new_prof = old_prof * numer_prof / below_prof

    prof_hi, prof_lo = split(new_prof)
    prof_two = jnp.concatenate([prof_hi, prof_lo], axis=0)
    for i in range(nx // 2):
        both = dot(prof_two, clean_hi[i], NT)
        part = both[0:32] + both[32:64] + dot(prof_hi, clean_lo[i], NT)
        part_send[:, 2 * i, :] = part[:, 0:ny]
        part_send[:, 2 * i + 1, :] = part[:, ny:2 * ny]
    for c in range(own):
        for d in ORDER:
            p = (ma + d) % GROUP
            copy(6, part_send.at[own * p + c], part_all.at[c, d - 1], z_peer(p), part_recv.at[c]).start()
        if c == 0:
            gram_c[ma] = pack_gram(dot(new_prof, jnp.concatenate([new_prof] * 4, axis=0), NT, HIGH))
            exchange(7, ma, z_peer, lambda p: gram_c.at[ma], gram_c)
    prof_new[...] = new_prof
    copy_new = pltpu.make_async_copy(prof_new, out_prof, local_sem.at[3])
    copy_new.start()

    arrive(7, ma, z_peer, gram_c)
    lane = lax.broadcasted_iota(jnp.int32, (8, 128), 1)
    block = ma // 2
    mask = jnp.logical_and(lane >= 32 * block, lane < 32 * block + 32)
    gram_rows = jnp.where(mask, total(gram_c), 0.0)
    for i in range(nx // 2):
        below = dot(gram_rows, jnp.concatenate([load_flat[i]] * 4, axis=0), NN, HIGH) + EPSILON
        below_all[:, 2 * i, :] = below[:, 0:ny]
        below_all[:, 2 * i + 1, :] = below[:, ny:2 * ny]

    for c in range(own):
        whole = part_all.at[c]
        copy(6, whole, whole, z_peer((ma + 1) % GROUP), part_recv.at[c]).wait_recv()
        k = own * ma + c
        value = part_send[k]
        for d in range(GROUP - 1):
            value = value + part_all[c, d]
        new_all[c] = load_in[k] * value / below_all[own * (ma % 2) + c]
        for p in range(GROUP):
            @pl.when(ma != p)
            def _():
                copy(8, new_all.at[c], out_load.at[k], z_peer(p)).start()
    copy_mine = pltpu.make_async_copy(new_all, out_load.at[pl.ds(own * ma, own)], local_sem.at[4])
    copy_mine.start()

    for i, (dx, dy) in enumerate(steps):
        @pl.when(exists(dx, dy))
        def _():
            halo(i, dx, dy).wait_send()
            sums(i, dx, dy).wait_send()
    sent(0, xc, xc_peer, gram_a)
    sent(1, ma, z_peer, bg_all)
    sent(2, y, y_peer, gram_b)
    sent(3, xc, xc_peer, prof_1)
    sent(4, y, y_peer, prof_2)
    sent(5, xc, xc_peer, prof_3)
    sent(7, ma, z_peer, gram_c)
    peer = z_peer((ma + 1) % GROUP)
    copy(6, part_all, part_all, peer).wait_send()
    copy_new.wait()
    copy_mine.wait()
    most = out_load.at[0:nk - own]
    copy(8, most, most, peer).wait_send()
    copy(8, most, most, peer).wait_recv()


def finish(load, prof, out_load, out_prof, sem):
    copies = [pltpu.make_async_copy(load, out_load, sem.at[0]), pltpu.make_async_copy(prof, out_prof, sem.at[1])]
    for c in copies:
        c.start()
    for c in copies:
        c.wait()


def per_device(spectra, loadings, profiles):
    nx, ny, nm = spectra.shape
    nk = loadings.shape[0]
    own = nk // GROUP
    wide_x, wide_y = nx + 2 * RADIUS, ny + 2 * SIDE
    anywhere = pl.BlockSpec(memory_space=pl.ANY)
    vmem = pltpu.VMEM
    held_load, held_prof = pl.pallas_call(
        kernel,
        out_shape=(
            pltpu.VMEM((nk, nx, ny), F32),
            pltpu.VMEM((nk, nm), F32),
        ),
        in_specs=[anywhere] * 3,
        out_specs=(anywhere, anywhere),
        scratch_shapes=[
            vmem((wide_x, wide_y, nm), BF16),
            vmem((nk, nx, ny), F32),
            vmem((nk, nm), F32),
            vmem((wide_x, ny, nm), F32),
            vmem((nx, ny, nm), F32),
            vmem((24, 3 * ny), F32),
            vmem((nx // 2, nk, 2 * ny), F32),
            vmem((nx // 2, 2 * nk, 2 * ny), BF16),
            vmem((nx // 2, 2 * ny, nm), BF16),
            vmem((nx // 2, 2 * ny, nm), BF16),
            vmem((GROUP, nx, ny), F32),
            vmem((GROUP, 8, 128), F32),
            vmem((GROUP, 8, 128), F32),
            vmem((GROUP, 8, 128), F32),
            vmem((GROUP, 8, 128), F32),
            vmem((GROUP, 8, 128), F32),
            vmem((GROUP, 8, 128), F32),
            vmem((nk, nm), F32),
            vmem((GROUP, 8, 128), F32),
            vmem((nk, nx, ny), F32),
            vmem((own, GROUP - 1, nx, ny), F32),
            vmem((8, nx, ny), F32),
            vmem((own, nx, ny), F32),
            vmem((128, 128), F32),
            vmem((nx, ny), F32),
            vmem((8, nx, ny), F32),
            vmem((2, 2 * nx, nm), BF16),
            vmem((2, 2 * nx + 32, nm), BF16),
            pltpu.SemaphoreType.DMA((5,)),
            pltpu.SemaphoreType.DMA((8,)),
            pltpu.SemaphoreType.DMA((8,)),
            pltpu.SemaphoreType.DMA((8,)),
            pltpu.SemaphoreType.DMA((8,)),
            pltpu.SemaphoreType.DMA((9,)),
            pltpu.SemaphoreType.DMA((9,)),
            pltpu.SemaphoreType.DMA((own,)),
        ],
        compiler_params=pltpu.CompilerParams(
            collective_id=0, has_side_effects=True, vmem_limit_bytes=60 * 1024 * 1024
        ),
    )(spectra, loadings, profiles)
    return pl.pallas_call(
        finish,
        out_shape=(
            jax.ShapeDtypeStruct((nk, nx, ny), F32),
            jax.ShapeDtypeStruct((nk, nm), F32),
        ),
        in_specs=[anywhere] * 2,
        out_specs=(anywhere, anywhere),
        scratch_shapes=[pltpu.SemaphoreType.DMA((2,))],
    )(*(pltpu.with_memory_space_constraint(a, pltpu.VMEM) for a in (held_load, held_prof)))


def solution(mesh):
    return jax.shard_map(
        per_device,
        mesh=mesh,
        in_specs=(P("gx", "gy", "ma"), P(None, "gx", "gy"), P(None, "ma")),
        out_specs=(P(None, "gx", "gy"), P(None, "ma")),
        check_vma=False,
    )
```

```python
import jax
import jax.numpy as jnp
import ml_dtypes
import numpy as np
from jax import lax
from jax.experimental import pallas as pl
from jax.experimental.pallas import tpu as pltpu
from jax.sharding import PartitionSpec as P

MESH = pl.DeviceIdType.MESH
F32 = jnp.float32
BF16 = jnp.bfloat16
HIGH = lax.Precision.HIGHEST

RADIUS = 2
SIDE = 16
GROUP = 8
EPSILON = 1e-06
CHUNKS = 2
ORDER = (4, 3, 5, 2, 6, 1, 7)

NT = (((1,), (1,)), ((), ()))
NN = (((1,), (0,)), ((), ()))


def taps():
    offsets = np.arange(-RADIUS, RADIUS + 1).astype(np.float32)
    raw = np.exp(-offsets * offsets / np.float32(2.0))
    return (raw / np.sum(raw)).astype(np.float32)


def split(value):
    high = value.astype(BF16)
    return high, (value - high.astype(F32)).astype(BF16)


def dot(a, b, dims, precision=None):
    return lax.dot_general(a, b, dims, precision=precision, preferred_element_type=F32)


def band(shape, shift, weights):
    row = lax.broadcasted_iota(jnp.int32, shape, 0)
    column = lax.broadcasted_iota(jnp.int32, shape, 1)
    at = column - row - shift
    out = jnp.zeros(shape, F32)
    for a in range(-RADIUS, RADIUS + 1):
        out = jnp.where(at == a, float(weights[a + RADIUS]), out)
    return out


def block_mask(b):
    lane = lax.broadcasted_iota(jnp.int32, (8, 128), 1)
    return jnp.logical_and(lane >= 32 * b, lane < 32 * (b + 1))


def pack_gram(full):
    out = jnp.zeros((8, 128), F32)
    for b in range(4):
        out = jnp.where(block_mask(b), full[8 * b:8 * b + 8, :], out)
    return out


def unpack_gram(packed):
    return jnp.concatenate([jnp.where(block_mask(b), packed, 0.0) for b in range(4)], axis=0)


def kernel(
    spectra, loadings, profiles, out_load, out_prof,
    ext, load_in, prof_in, ysm, smooth, rows, load_flat, load_split, clean_hi, clean_lo,
    bg_all, gram_a, gram_b, prof_send, prof_1, prof_2, prof_3, prof_new,
    gram_c, part_send, part_all, below_all, new_all, pad_t,
    sums_own, sums_in, edge_own, edge_in, local_sem, sums_send, sums_recv, halo_send, halo_recv, send_sem, recv_sem, part_recv,
):
    nx, ny, nm = spectra.shape
    nk = loadings.shape[0]
    size = nk // GROUP // CHUNKS
    own = nk // GROUP
    gx, gy, ma = lax.axis_index("gx"), lax.axis_index("gy"), lax.axis_index("ma")
    count_x, count_y = lax.axis_size("gx"), lax.axis_size("gy")
    half, y = gy // GROUP, gy % GROUP
    xc = gx * 2 + half
    weights = taps()

    def z_peer(p):
        return {"gx": gx, "gy": gy, "ma": p}

    def y_peer(p):
        return {"gx": gx, "gy": half * GROUP + p, "ma": ma}

    def xc_peer(p):
        return {"gx": p // 2, "gy": (p % 2) * GROUP + y, "ma": ma}

    copy_spectra = pltpu.make_async_copy(
        spectra, ext.at[RADIUS:RADIUS + nx, SIDE:SIDE + ny, :], local_sem.at[0]
    )
    copy_load = pltpu.make_async_copy(loadings, load_in, local_sem.at[1])
    copy_prof = pltpu.make_async_copy(profiles, prof_in, local_sem.at[2])
    copy_spectra.start()
    copy_load.start()
    copy_prof.start()

    has = {
        ("x", -1): gx > 0, ("x", 0): None, ("x", 1): gx < count_x - 1,
        ("y", -1): gy > 0, ("y", 0): None, ("y", 1): gy < count_y - 1,
    }
    steps = [(-1, 0), (1, 0), (0, -1), (0, 1), (-1, -1), (-1, 1), (1, -1), (1, 1)]

    def exists(dx, dy):
        a, b = has[("x", dx)], has[("y", dy)]
        if a is None:
            return b
        if b is None:
            return a
        return jnp.logical_and(a, b)

    rows_out = {-1: slice(0, 16), 0: slice(0, 2 * nx), 1: slice(2 * nx - 16, 2 * nx)}
    rows_land = {-1: slice(16 + 2 * nx, 32 + 2 * nx), 0: slice(16, 16 + 2 * nx), 1: slice(0, 16)}
    middle = slice(SIDE, SIDE + ny)

    def halo_refs(dx, dy):
        if dy == 0:
            first, land = (RADIUS, nx + RADIUS) if dx < 0 else (nx, 0)
            return ext.at[first:first + RADIUS, middle, :], ext.at[land:land + RADIUS, middle, :]
        side = (dy + 1) // 2
        return edge_own.at[side, rows_out[dx], :], edge_in.at[1 - side, rows_land[dx], :]

    def halo(i, dx, dy):
        source, target = halo_refs(dx, dy)
        return pltpu.make_async_remote_copy(
            src_ref=source,
            dst_ref=target,
            send_sem=halo_send.at[i],
            recv_sem=halo_recv.at[i],
            device_id={"gx": gx + dx, "gy": gy + dy, "ma": ma},
            device_id_type=MESH,
        )

    barrier = pltpu.get_barrier_semaphore()
    for dx, dy in steps:
        @pl.when(exists(dx, dy))
        def _():
            pl.semaphore_signal(
                barrier, inc=1, device_id={"gx": gx + dx, "gy": gy + dy, "ma": ma}, device_id_type=MESH
            )
    for d in ORDER:
        for to in (z_peer((ma + d) % GROUP), y_peer((y + d) % GROUP), xc_peer((xc + d) % GROUP)):
            pl.semaphore_signal(barrier, inc=1, device_id=to, device_id_type=MESH)

    copy_spectra.wait()
    ones = jnp.ones((8, nm), BF16)
    for x in range(nx):
        sums_own[x:x + 1, :] = dot(ones, ext[RADIUS + x, SIDE:SIDE + ny, :], NT)[0:1, :]

    near_x = (gx > 0).astype(jnp.int32) + (gx < count_x - 1).astype(jnp.int32)
    near_y = (gy > 0).astype(jnp.int32) + (gy < count_y - 1).astype(jnp.int32)
    pl.semaphore_wait(barrier, 3 * (GROUP - 1) + near_x + near_y + near_x * near_y)

    def sums(i, dx, dy):
        return pltpu.make_async_remote_copy(
            src_ref=sums_own,
            dst_ref=sums_in.at[i],
            send_sem=sums_send.at[i],
            recv_sem=sums_recv.at[i],
            device_id={"gx": gx + dx, "gy": gy + dy, "ma": ma},
            device_id_type=MESH,
        )

    def start(make, chosen):
        for i, (dx, dy) in enumerate(steps):
            if chosen(dy):
                @pl.when(exists(dx, dy))
                def _():
                    make(i, dx, dy).start()

    start(sums, lambda dy: True)
    start(halo, lambda dy: dy == 0)
    at = lax.broadcasted_iota(jnp.int32, (2 * nx, 16 * nx), 0)
    column = lax.broadcasted_iota(jnp.int32, (2 * nx, 16 * nx), 1)
    for side, first in ((0, SIDE), (1, SIDE + ny - 16)):
        tile = ext[RADIUS:RADIUS + nx, first:first + 16, :].reshape(16 * nx, nm)
        pick = column == 16 * (at >> 1) + (at & 1) + side * (16 - RADIUS)
        edge_own[side] = dot(jnp.where(pick, 1.0, 0.0).astype(BF16), tile, NN).astype(BF16)
    start(halo, lambda dy: dy != 0)

    def copy(stage, source, target, device, recv=None):
        return pltpu.make_async_remote_copy(
            src_ref=source,
            dst_ref=target,
            send_sem=send_sem.at[stage],
            recv_sem=recv_sem.at[stage] if recv is None else recv,
            device_id=device,
            device_id_type=MESH,
        )

    def exchange(stage, me, peer_id, source, slots):
        for d in ORDER:
            p = (me + d) % GROUP
            copy(stage, source(p), slots.at[me], peer_id(p)).start()

    def arrive(stage, me, peer_id, slots):
        whole = slots.at[0:GROUP - 1]
        copy(stage, whole, whole, peer_id((me + 1) % GROUP)).wait_recv()

    def sent(stage, me, peer_id, slots):
        whole = slots.at[0:GROUP - 1]
        copy(stage, whole, whole, peer_id((me + 1) % GROUP)).wait_send()

    def total(slots):
        out = slots[0]
        for p in range(1, GROUP):
            out = out + slots[p]
        return out

    for dx, dy in steps:
        @pl.when(jnp.logical_not(exists(-dx, -dy)))
        def _():
            unused, target = halo_refs(dx, dy)
            target[...] = jnp.zeros(target.shape, BF16)

    copy_load.wait()
    for x in range(nx):
        load_flat[x // 2, :, 128 * (x % 2):128 * (x % 2) + 128] = load_in[:, x, :]
    full = jnp.zeros((32, 128), F32)
    for i in range(nx // 2):
        part = load_flat[i]
        high, low = split(part)
        load_split[i, 0:32, :] = high
        load_split[i, 32:64, :] = low
        full = full + dot(part, jnp.concatenate([part] * 4, axis=0), NT, HIGH)
    gram_a[xc] = pack_gram(full)
    exchange(0, xc, xc_peer, lambda p: gram_a.at[xc], gram_a)

    for i, (dx, dy) in enumerate(steps):
        there = exists(-dx, -dy)

        @pl.when(there)
        def _():
            sums(i, dx, dy).wait_recv()

        @pl.when(jnp.logical_not(there))
        def _():
            sums_in[i] = jnp.zeros_like(sums_own)
    for side in (-1, 0, 1):
        columns = slice(ny * (side + 1), ny * (side + 2))
        low, high = steps.index((1, -side)), steps.index((-1, -side))
        rows[0:RADIUS, columns] = sums_in[low, nx - RADIUS:nx, :]
        rows[RADIUS:nx + RADIUS, columns] = sums_own[...] if side == 0 else sums_in[steps.index((0, -side))]
        rows[nx + RADIUS:nx + 2 * RADIUS, columns] = sums_in[high, 0:RADIUS, :]

    hi_taps = weights.astype(ml_dtypes.bfloat16).astype(np.float32)
    lo_taps = (weights - hi_taps).astype(ml_dtypes.bfloat16).astype(np.float32)
    wide = (ny, ny + 2 * SIDE)
    both_taps = hi_taps + lo_taps
    w0, w1, w2 = (float(weights[RADIUS + a]) for a in range(3))
    row_x = (
        w0 * rows[2:nx + 2, :] + w1 * (rows[1:nx + 1, :] + rows[3:nx + 3, :])
        + w2 * (rows[0:nx, :] + rows[4:nx + 4, :])
    )
    bg_all[ma] = dot(row_x, band((ny, 3 * ny), ny, both_taps), NT, HIGH)
    exchange(1, ma, z_peer, lambda p: bg_all.at[ma], bg_all)

    arrive(0, xc, xc_peer, gram_a)
    gram_b[y] = total(gram_a)
    exchange(2, y, y_peer, lambda p: gram_b.at[y], gram_b)
    band_two = jnp.concatenate(
        [band(wide, SIDE, hi_taps), band(wide, SIDE, lo_taps)], axis=0
    ).astype(BF16)
    for i, (dx, dy) in enumerate(steps):
        @pl.when(exists(-dx, -dy))
        def _():
            halo(i, dx, dy).wait_recv()
    at = lax.broadcasted_iota(jnp.int32, (16 * (nx + 2 * RADIUS), edge_in.shape[1]), 0)
    column = lax.broadcasted_iota(jnp.int32, (16 * (nx + 2 * RADIUS), edge_in.shape[1]), 1)
    for side, first in ((0, SIDE - 16), (1, SIDE + ny)):
        inside = (at & 15) - (16 - RADIUS) * (1 - side)
        pick = jnp.logical_and(
            column == 12 + 2 * (at >> 4) + inside, jnp.logical_and(inside >= 0, inside < RADIUS)
        )
        spread = dot(jnp.where(pick, 1.0, 0.0).astype(BF16), edge_in[side], NN).astype(BF16)
        ext[:, first:first + 16, :] = spread.reshape(nx + 2 * RADIUS, 16, nm)

    @pl.loop(0, (nx + 2 * RADIUS) // 4)
    def _(i):
        for j in range(4):
            x = 4 * i + j
            both = dot(band_two, ext[x], NN)
            ysm[x] = both[0:ny] + both[ny:2 * ny]

    @pl.loop(0, nx // 2)
    def _(i):
        for j in range(2):
            x = 2 * i + j
            smooth[x] = (
                w0 * ysm[x + 2] + w1 * (ysm[x + 1] + ysm[x + 3]) + w2 * (ysm[x] + ysm[x + 4])
            )

    copy_prof.wait()
    arrive(2, y, y_peer, gram_b)
    gram = unpack_gram(total(gram_b))
    old_prof = prof_in[...]
    below_prof = dot(gram, jnp.concatenate([old_prof] * 4, axis=0), NN, HIGH) + EPSILON

    arrive(1, ma, z_peer, bg_all)
    pad_t[0:nx, :] = total(bg_all) * (1.0 / 2048.0)
    back = pad_t[...].T

    acc = jnp.zeros((64, 256), F32)
    acc_lo = jnp.zeros((32, 256), F32)
    for i in range(nx // 2):
        for j in range(2):
            x = 2 * i + j
            value = jnp.maximum(smooth[x] - back[:, x:x + 1], 0.0)
            high, low = split(value)
            clean_hi[i, ny * j:ny * j + ny, :] = high
            clean_lo[i, ny * j:ny * j + ny, :] = low
        acc = acc + dot(load_split[i], clean_hi[i], NN)
        acc_lo = acc_lo + dot(load_split[i, 0:32, :], clean_lo[i], NN)
    numer = acc[0:32] + acc[32:64] + acc_lo

    for p in range(GROUP):
        prof_send[p] = numer[8 * (p // 2):8 * (p // 2) + 8, 128 * (p % 2):128 * (p % 2) + 128]
    exchange(3, xc, xc_peer, lambda p: prof_send.at[p], prof_1)
    prof_1[xc] = prof_send[xc]
    arrive(3, xc, xc_peer, prof_1)
    prof_2[y] = total(prof_1)
    exchange(4, y, y_peer, lambda p: prof_2.at[y], prof_2)
    arrive(4, y, y_peer, prof_2)
    prof_3[xc] = total(prof_2)
    exchange(5, xc, xc_peer, lambda p: prof_3.at[xc], prof_3)
    arrive(5, xc, xc_peer, prof_3)
    numer_prof = jnp.concatenate(
        [jnp.concatenate([prof_3[2 * b], prof_3[2 * b + 1]], axis=1) for b in range(4)], axis=0
    )
    new_prof = old_prof * numer_prof / below_prof

    prof_hi, prof_lo = split(new_prof)
    prof_two = jnp.concatenate([prof_hi, prof_lo], axis=0)
    for i in range(nx // 2):
        both = dot(prof_two, clean_hi[i], NT)
        part = both[0:32] + both[32:64] + dot(prof_hi, clean_lo[i], NT)
        part_send[:, 2 * i, :] = part[:, 0:ny]
        part_send[:, 2 * i + 1, :] = part[:, ny:2 * ny]
    for c in range(CHUNKS):
        for d in ORDER:
            p = (ma + d) % GROUP
            source = part_send.at[pl.ds(own * p + size * c, size)]
            copy(6, source, part_all.at[c, d - 1], z_peer(p), part_recv.at[c]).start()
        if c == 0:
            gram_c[ma] = pack_gram(dot(new_prof, jnp.concatenate([new_prof] * 4, axis=0), NT, HIGH))
            exchange(7, ma, z_peer, lambda p: gram_c.at[ma], gram_c)
    prof_new[...] = new_prof
    copy_new = pltpu.make_async_copy(prof_new, out_prof, local_sem.at[3])
    copy_new.start()

    arrive(7, ma, z_peer, gram_c)
    lane = lax.broadcasted_iota(jnp.int32, (8, 128), 1)
    block = ma // 2
    mask = jnp.logical_and(lane >= 32 * block, lane < 32 * block + 32)
    gram_rows = jnp.where(mask, total(gram_c), 0.0)
    for i in range(nx // 2):
        below = dot(gram_rows, jnp.concatenate([load_flat[i]] * 4, axis=0), NN, HIGH) + EPSILON
        below_all[:, 2 * i, :] = below[:, 0:ny]
        below_all[:, 2 * i + 1, :] = below[:, ny:2 * ny]

    for c in range(CHUNKS):
        whole = part_all.at[c]
        copy(6, whole, whole, z_peer((ma + 1) % GROUP), part_recv.at[c]).wait_recv()
        k = own * ma + size * c
        value = part_send[pl.ds(k, size)]
        for d in range(GROUP - 1):
            value = value + part_all[c, d]
        below = below_all[pl.ds(own * (ma % 2) + size * c, size)]
        new_all[c] = load_in[pl.ds(k, size)] * value / below
        for p in range(GROUP):
            @pl.when(ma != p)
            def _():
                copy(8, new_all.at[c], out_load.at[pl.ds(k, size)], z_peer(p)).start()
    mine = [
        pltpu.make_async_copy(
            new_all.at[c], out_load.at[pl.ds(own * ma + size * c, size)], local_sem.at[4 + c]
        )
        for c in range(CHUNKS)
    ]
    for part in mine:
        part.start()

    for i, (dx, dy) in enumerate(steps):
        @pl.when(exists(dx, dy))
        def _():
            halo(i, dx, dy).wait_send()
            sums(i, dx, dy).wait_send()
    sent(0, xc, xc_peer, gram_a)
    sent(1, ma, z_peer, bg_all)
    sent(2, y, y_peer, gram_b)
    sent(3, xc, xc_peer, prof_1)
    sent(4, y, y_peer, prof_2)
    sent(5, xc, xc_peer, prof_3)
    sent(7, ma, z_peer, gram_c)
    peer = z_peer((ma + 1) % GROUP)
    copy(6, part_all, part_all, peer).wait_send()
    copy_new.wait()
    for part in mine:
        part.wait()
    most = out_load.at[0:nk - own]
    copy(8, most, most, peer).wait_send()
    copy(8, most, most, peer).wait_recv()


def finish(load, prof, out_load, out_prof, sem):
    copies = [pltpu.make_async_copy(load, out_load, sem.at[0]), pltpu.make_async_copy(prof, out_prof, sem.at[1])]
    for c in copies:
        c.start()
    for c in copies:
        c.wait()


def per_device(spectra, loadings, profiles):
    nx, ny, nm = spectra.shape
    nk = loadings.shape[0]
    own = nk // GROUP
    wide_x, wide_y = nx + 2 * RADIUS, ny + 2 * SIDE
    anywhere = pl.BlockSpec(memory_space=pl.ANY)
    vmem = pltpu.VMEM
    held_load, held_prof = pl.pallas_call(
        kernel,
        out_shape=(
            pltpu.VMEM((nk, nx, ny), F32),
            pltpu.VMEM((nk, nm), F32),
        ),
        in_specs=[anywhere] * 3,
        out_specs=(anywhere, anywhere),
        scratch_shapes=[
            vmem((wide_x, wide_y, nm), BF16),
            vmem((nk, nx, ny), F32),
            vmem((nk, nm), F32),
            vmem((wide_x, ny, nm), F32),
            vmem((nx, ny, nm), F32),
            vmem((24, 3 * ny), F32),
            vmem((nx // 2, nk, 2 * ny), F32),
            vmem((nx // 2, 2 * nk, 2 * ny), BF16),
            vmem((nx // 2, 2 * ny, nm), BF16),
            vmem((nx // 2, 2 * ny, nm), BF16),
            vmem((GROUP, nx, ny), F32),
            vmem((GROUP, 8, 128), F32),
            vmem((GROUP, 8, 128), F32),
            vmem((GROUP, 8, 128), F32),
            vmem((GROUP, 8, 128), F32),
            vmem((GROUP, 8, 128), F32),
            vmem((GROUP, 8, 128), F32),
            vmem((nk, nm), F32),
            vmem((GROUP, 8, 128), F32),
            vmem((nk, nx, ny), F32),
            vmem((CHUNKS, GROUP - 1, own // CHUNKS, nx, ny), F32),
            vmem((8, nx, ny), F32),
            vmem((CHUNKS, own // CHUNKS, nx, ny), F32),
            vmem((128, 128), F32),
            vmem((nx, ny), F32),
            vmem((8, nx, ny), F32),
            vmem((2, 2 * nx, nm), BF16),
            vmem((2, 2 * nx + 32, nm), BF16),
            pltpu.SemaphoreType.DMA((4 + CHUNKS,)),
            pltpu.SemaphoreType.DMA((8,)),
            pltpu.SemaphoreType.DMA((8,)),
            pltpu.SemaphoreType.DMA((8,)),
            pltpu.SemaphoreType.DMA((8,)),
            pltpu.SemaphoreType.DMA((9,)),
            pltpu.SemaphoreType.DMA((9,)),
            pltpu.SemaphoreType.DMA((CHUNKS,)),
        ],
        compiler_params=pltpu.CompilerParams(
            collective_id=0, has_side_effects=True, vmem_limit_bytes=60 * 1024 * 1024
        ),
    )(spectra, loadings, profiles)
    return pl.pallas_call(
        finish,
        out_shape=(
            jax.ShapeDtypeStruct((nk, nx, ny), F32),
            jax.ShapeDtypeStruct((nk, nm), F32),
        ),
        in_specs=[anywhere] * 2,
        out_specs=(anywhere, anywhere),
        scratch_shapes=[pltpu.SemaphoreType.DMA((2,))],
    )(*(pltpu.with_memory_space_constraint(a, pltpu.VMEM) for a in (held_load, held_prof)))


def solution(mesh):
    return jax.shard_map(
        per_device,
        mesh=mesh,
        in_specs=(P("gx", "gy", "ma"), P(None, "gx", "gy"), P(None, "ma")),
        out_specs=(P(None, "gx", "gy"), P(None, "ma")),
        check_vma=False,
    )
```

```python
import jax
import jax.numpy as jnp
import ml_dtypes
import numpy as np
from jax import lax
from jax.experimental import pallas as pl
from jax.experimental.pallas import tpu as pltpu
from jax.sharding import PartitionSpec as P

MESH = pl.DeviceIdType.MESH
F32 = jnp.float32
BF16 = jnp.bfloat16
HIGH = lax.Precision.HIGHEST

RADIUS = 2
SIDE = 16
GROUP = 8
EPSILON = 1e-06
CHUNKS = 2
ORDER = (4, 3, 5, 2, 6, 1, 7)

NT = (((1,), (1,)), ((), ()))
NN = (((1,), (0,)), ((), ()))


def taps():
    offsets = np.arange(-RADIUS, RADIUS + 1).astype(np.float32)
    raw = np.exp(-offsets * offsets / np.float32(2.0))
    return (raw / np.sum(raw)).astype(np.float32)


def split(value):
    high = value.astype(BF16)
    return high, (value - high.astype(F32)).astype(BF16)


def dot(a, b, dims, precision=None):
    return lax.dot_general(a, b, dims, precision=precision, preferred_element_type=F32)


def band(shape, shift, weights):
    row = lax.broadcasted_iota(jnp.int32, shape, 0)
    column = lax.broadcasted_iota(jnp.int32, shape, 1)
    at = column - row - shift
    out = jnp.zeros(shape, F32)
    for a in range(-RADIUS, RADIUS + 1):
        out = jnp.where(at == a, float(weights[a + RADIUS]), out)
    return out


def block_mask(b):
    lane = lax.broadcasted_iota(jnp.int32, (8, 128), 1)
    return jnp.logical_and(lane >= 32 * b, lane < 32 * (b + 1))


def pack_gram(full):
    out = jnp.zeros((8, 128), F32)
    for b in range(4):
        out = jnp.where(block_mask(b), full[8 * b:8 * b + 8, :], out)
    return out


def unpack_gram(packed):
    return jnp.concatenate([jnp.where(block_mask(b), packed, 0.0) for b in range(4)], axis=0)


def kernel(
    spectra, loadings, profiles, out_load, out_prof,
    ext, load_in, prof_in, ysm, smooth, rows, load_flat, load_split, clean_hi, clean_lo,
    bg_all, gram_a, gram_b, prof_send, prof_1, prof_2, prof_3, prof_new,
    gram_c, part_send, part_all, below_all, new_all, pad_t,
    band_bg, sums_own, sums_in, edge_own, edge_in, local_sem, sums_send, sums_recv, halo_send, halo_recv, send_sem, recv_sem, part_recv, heard,
):
    nx, ny, nm = spectra.shape
    nk = loadings.shape[0]
    size = nk // GROUP // CHUNKS
    own = nk // GROUP
    gx, gy, ma = lax.axis_index("gx"), lax.axis_index("gy"), lax.axis_index("ma")
    count_x, count_y = lax.axis_size("gx"), lax.axis_size("gy")
    half, y = gy // GROUP, gy % GROUP
    xc = gx * 2 + half
    weights = taps()

    def z_peer(p):
        return {"gx": gx, "gy": gy, "ma": p}

    def y_peer(p):
        return {"gx": gx, "gy": half * GROUP + p, "ma": ma}

    def xc_peer(p):
        return {"gx": p // 2, "gy": (p % 2) * GROUP + y, "ma": ma}

    copy_spectra = pltpu.make_async_copy(
        spectra, ext.at[RADIUS:RADIUS + nx, SIDE:SIDE + ny, :], local_sem.at[0]
    )
    copy_load = pltpu.make_async_copy(loadings, load_in, local_sem.at[1])
    copy_prof = pltpu.make_async_copy(profiles, prof_in, local_sem.at[2])
    copy_spectra.start()
    copy_load.start()
    copy_prof.start()

    has = {
        ("x", -1): gx > 0, ("x", 0): None, ("x", 1): gx < count_x - 1,
        ("y", -1): gy > 0, ("y", 0): None, ("y", 1): gy < count_y - 1,
    }
    steps = [(-1, 0), (1, 0), (0, -1), (0, 1), (-1, -1), (-1, 1), (1, -1), (1, 1)]

    def exists(dx, dy):
        a, b = has[("x", dx)], has[("y", dy)]
        if a is None:
            return b
        if b is None:
            return a
        return jnp.logical_and(a, b)

    rows_out = {-1: slice(0, 16), 0: slice(0, 2 * nx), 1: slice(2 * nx - 16, 2 * nx)}
    rows_land = {-1: slice(16 + 2 * nx, 32 + 2 * nx), 0: slice(16, 16 + 2 * nx), 1: slice(0, 16)}
    middle = slice(SIDE, SIDE + ny)

    def halo_refs(dx, dy):
        if dy == 0:
            first, land = (RADIUS, nx + RADIUS) if dx < 0 else (nx, 0)
            return ext.at[first:first + RADIUS, middle, :], ext.at[land:land + RADIUS, middle, :]
        side = (dy + 1) // 2
        return edge_own.at[side, rows_out[dx], :], edge_in.at[1 - side, rows_land[dx], :]

    def halo(i, dx, dy):
        source, target = halo_refs(dx, dy)
        return pltpu.make_async_remote_copy(
            src_ref=source,
            dst_ref=target,
            send_sem=halo_send.at[i],
            recv_sem=halo_recv.at[i],
            device_id={"gx": gx + dx, "gy": gy + dy, "ma": ma},
            device_id_type=MESH,
        )

    barrier = pltpu.get_barrier_semaphore()
    for dx, dy in steps:
        @pl.when(exists(dx, dy))
        def _():
            pl.semaphore_signal(
                barrier, inc=1, device_id={"gx": gx + dx, "gy": gy + dy, "ma": ma}, device_id_type=MESH
            )
    for d in ORDER:
        far = d == GROUP // 2
        near = () if far else (z_peer((ma + d) % GROUP), y_peer((y + d) % GROUP))
        for to in (*near, xc_peer((xc + d) % GROUP)):
            pl.semaphore_signal(barrier, inc=1, device_id=to, device_id_type=MESH)

    copy_spectra.wait()
    ones = jnp.ones((8, nm), BF16)
    for x in range(nx):
        sums_own[x:x + 1, :] = dot(ones, ext[RADIUS + x, SIDE:SIDE + ny, :], NT)[0:1, :]

    hi_taps = weights.astype(ml_dtypes.bfloat16).astype(np.float32)
    lo_taps = (weights - hi_taps).astype(ml_dtypes.bfloat16).astype(np.float32)
    band_bg[...] = band((ny, 3 * ny), ny, hi_taps + lo_taps)

    near_x = (gx > 0).astype(jnp.int32) + (gx < count_x - 1).astype(jnp.int32)
    near_y = (gy > 0).astype(jnp.int32) + (gy < count_y - 1).astype(jnp.int32)
    pl.semaphore_wait(barrier, 3 * (GROUP - 1) - 2 + near_x + near_y + near_x * near_y)

    def sums(i, dx, dy):
        return pltpu.make_async_remote_copy(
            src_ref=sums_own,
            dst_ref=sums_in.at[i],
            send_sem=sums_send.at[i],
            recv_sem=sums_recv.at[i],
            device_id={"gx": gx + dx, "gy": gy + dy, "ma": ma},
            device_id_type=MESH,
        )

    def start(make, chosen):
        for i, (dx, dy) in enumerate(steps):
            if chosen(dy):
                @pl.when(exists(dx, dy))
                def _():
                    make(i, dx, dy).start()

    start(sums, lambda dy: True)
    before_y, before_z = y_peer((y + GROUP - 1) % GROUP), z_peer((ma + GROUP - 1) % GROUP)
    for sem, to in ((0, before_y), (1, before_z)):
        pl.semaphore_signal(heard.at[sem], inc=1, device_id=to, device_id_type=MESH)
    start(halo, lambda dy: dy == 0)
    at = lax.broadcasted_iota(jnp.int32, (2 * nx, 16 * nx), 0)
    column = lax.broadcasted_iota(jnp.int32, (2 * nx, 16 * nx), 1)
    for side, first in ((0, SIDE), (1, SIDE + ny - 16)):
        tile = ext[RADIUS:RADIUS + nx, first:first + 16, :].reshape(16 * nx, nm)
        pick = column == 16 * (at >> 1) + (at & 1) + side * (16 - RADIUS)
        edge_own[side] = dot(jnp.where(pick, 1.0, 0.0).astype(BF16), tile, NN).astype(BF16)
    start(halo, lambda dy: dy != 0)

    def copy(stage, source, target, device, recv=None):
        return pltpu.make_async_remote_copy(
            src_ref=source,
            dst_ref=target,
            send_sem=send_sem.at[stage],
            recv_sem=recv_sem.at[stage] if recv is None else recv,
            device_id=device,
            device_id_type=MESH,
        )

    def exchange(stage, me, peer_id, source, slots):
        for d in ORDER:
            p = (me + d) % GROUP
            copy(stage, source(p), slots.at[me], peer_id(p)).start()

    def arrive(stage, me, peer_id, slots):
        whole = slots.at[0:GROUP - 1]
        copy(stage, whole, whole, peer_id((me + 1) % GROUP)).wait_recv()

    def sent(stage, me, peer_id, slots):
        whole = slots.at[0:GROUP - 1]
        copy(stage, whole, whole, peer_id((me + 1) % GROUP)).wait_send()

    def total(slots):
        out = slots[0]
        for p in range(1, GROUP):
            out = out + slots[p]
        return out

    for dx, dy in steps:
        @pl.when(jnp.logical_not(exists(-dx, -dy)))
        def _():
            unused, target = halo_refs(dx, dy)
            target[...] = jnp.zeros(target.shape, BF16)

    copy_load.wait()
    for x in range(nx):
        load_flat[x // 2, :, 128 * (x % 2):128 * (x % 2) + 128] = load_in[:, x, :]
    full = jnp.zeros((32, 128), F32)
    for i in range(nx // 2):
        part = load_flat[i]
        high, low = split(part)
        load_split[i, 0:32, :] = high
        load_split[i, 32:64, :] = low
        full = full + dot(part, jnp.concatenate([part] * 4, axis=0), NT, HIGH)
    gram_a[xc] = pack_gram(full)
    exchange(0, xc, xc_peer, lambda p: gram_a.at[xc], gram_a)

    for i, (dx, dy) in enumerate(steps):
        there = exists(-dx, -dy)

        @pl.when(there)
        def _():
            sums(i, dx, dy).wait_recv()

        @pl.when(jnp.logical_not(there))
        def _():
            sums_in[i] = jnp.zeros_like(sums_own)
    for side in (-1, 0, 1):
        columns = slice(ny * (side + 1), ny * (side + 2))
        low, high = steps.index((1, -side)), steps.index((-1, -side))
        rows[0:RADIUS, columns] = sums_in[low, nx - RADIUS:nx, :]
        rows[RADIUS:nx + RADIUS, columns] = sums_own[...] if side == 0 else sums_in[steps.index((0, -side))]
        rows[nx + RADIUS:nx + 2 * RADIUS, columns] = sums_in[high, 0:RADIUS, :]

    wide = (ny, ny + 2 * SIDE)
    w0, w1, w2 = (float(weights[RADIUS + a]) for a in range(3))
    row_x = (
        w0 * rows[2:nx + 2, :] + w1 * (rows[1:nx + 1, :] + rows[3:nx + 3, :])
        + w2 * (rows[0:nx, :] + rows[4:nx + 4, :])
    )
    bg_all[ma] = dot(row_x, band_bg[...], NT, HIGH)
    pl.semaphore_wait(heard.at[1], 1)
    exchange(1, ma, z_peer, lambda p: bg_all.at[ma], bg_all)

    arrive(0, xc, xc_peer, gram_a)
    gram_b[y] = total(gram_a)
    pl.semaphore_wait(heard.at[0], 1)
    exchange(2, y, y_peer, lambda p: gram_b.at[y], gram_b)
    band_two = jnp.concatenate(
        [band(wide, SIDE, hi_taps), band(wide, SIDE, lo_taps)], axis=0
    ).astype(BF16)
    for i, (dx, dy) in enumerate(steps):
        @pl.when(exists(-dx, -dy))
        def _():
            halo(i, dx, dy).wait_recv()
    at = lax.broadcasted_iota(jnp.int32, (16 * (nx + 2 * RADIUS), edge_in.shape[1]), 0)
    column = lax.broadcasted_iota(jnp.int32, (16 * (nx + 2 * RADIUS), edge_in.shape[1]), 1)
    for side, first in ((0, SIDE - 16), (1, SIDE + ny)):
        inside = (at & 15) - (16 - RADIUS) * (1 - side)
        pick = jnp.logical_and(
            column == 12 + 2 * (at >> 4) + inside, jnp.logical_and(inside >= 0, inside < RADIUS)
        )
        spread = dot(jnp.where(pick, 1.0, 0.0).astype(BF16), edge_in[side], NN).astype(BF16)
        ext[:, first:first + 16, :] = spread.reshape(nx + 2 * RADIUS, 16, nm)

    @pl.loop(0, (nx + 2 * RADIUS) // 4)
    def _(i):
        for j in range(4):
            x = 4 * i + j
            both = dot(band_two, ext[x], NN)
            ysm[x] = both[0:ny] + both[ny:2 * ny]

    @pl.loop(0, nx // 2)
    def _(i):
        for j in range(2):
            x = 2 * i + j
            smooth[x] = (
                w0 * ysm[x + 2] + w1 * (ysm[x + 1] + ysm[x + 3]) + w2 * (ysm[x] + ysm[x + 4])
            )

    copy_prof.wait()
    arrive(2, y, y_peer, gram_b)
    gram = unpack_gram(total(gram_b))
    old_prof = prof_in[...]
    below_prof = dot(gram, jnp.concatenate([old_prof] * 4, axis=0), NN, HIGH) + EPSILON

    arrive(1, ma, z_peer, bg_all)
    pad_t[0:nx, :] = total(bg_all) * (1.0 / 2048.0)
    back = pad_t[...].T

    acc = jnp.zeros((64, 256), F32)
    acc_lo = jnp.zeros((32, 256), F32)
    for i in range(nx // 2):
        for j in range(2):
            x = 2 * i + j
            value = jnp.maximum(smooth[x] - back[:, x:x + 1], 0.0)
            high, low = split(value)
            clean_hi[i, ny * j:ny * j + ny, :] = high
            clean_lo[i, ny * j:ny * j + ny, :] = low
        acc = acc + dot(load_split[i], clean_hi[i], NN)
        acc_lo = acc_lo + dot(load_split[i, 0:32, :], clean_lo[i], NN)
    numer = acc[0:32] + acc[32:64] + acc_lo

    for p in range(GROUP):
        prof_send[p] = numer[8 * (p // 2):8 * (p // 2) + 8, 128 * (p % 2):128 * (p % 2) + 128]
    exchange(3, xc, xc_peer, lambda p: prof_send.at[p], prof_1)
    prof_1[xc] = prof_send[xc]
    arrive(3, xc, xc_peer, prof_1)
    prof_2[y] = total(prof_1)
    exchange(4, y, y_peer, lambda p: prof_2.at[y], prof_2)
    arrive(4, y, y_peer, prof_2)
    prof_3[xc] = total(prof_2)
    exchange(5, xc, xc_peer, lambda p: prof_3.at[xc], prof_3)
    arrive(5, xc, xc_peer, prof_3)
    numer_prof = jnp.concatenate(
        [jnp.concatenate([prof_3[2 * b], prof_3[2 * b + 1]], axis=1) for b in range(4)], axis=0
    )
    new_prof = old_prof * numer_prof / below_prof

    prof_hi, prof_lo = split(new_prof)
    prof_two = jnp.concatenate([prof_hi, prof_lo], axis=0)
    for i in range(nx // 2):
        both = dot(prof_two, clean_hi[i], NT)
        part = both[0:32] + both[32:64] + dot(prof_hi, clean_lo[i], NT)
        part_send[:, 2 * i, :] = part[:, 0:ny]
        part_send[:, 2 * i + 1, :] = part[:, ny:2 * ny]
    for c in range(CHUNKS):
        for d in ORDER:
            p = (ma + d) % GROUP
            source = part_send.at[pl.ds(own * p + size * c, size)]
            copy(6, source, part_all.at[c, d - 1], z_peer(p), part_recv.at[c]).start()
        if c == 0:
            gram_c[ma] = pack_gram(dot(new_prof, jnp.concatenate([new_prof] * 4, axis=0), NT, HIGH))
            exchange(7, ma, z_peer, lambda p: gram_c.at[ma], gram_c)
    prof_new[...] = new_prof
    copy_new = pltpu.make_async_copy(prof_new, out_prof, local_sem.at[3])
    copy_new.start()

    arrive(7, ma, z_peer, gram_c)
    lane = lax.broadcasted_iota(jnp.int32, (8, 128), 1)
    block = ma // 2
    mask = jnp.logical_and(lane >= 32 * block, lane < 32 * block + 32)
    gram_rows = jnp.where(mask, total(gram_c), 0.0)
    for i in range(nx // 2):
        below = dot(gram_rows, jnp.concatenate([load_flat[i]] * 4, axis=0), NN, HIGH) + EPSILON
        below_all[:, 2 * i, :] = below[:, 0:ny]
        below_all[:, 2 * i + 1, :] = below[:, ny:2 * ny]

    for c in range(CHUNKS):
        whole = part_all.at[c]
        copy(6, whole, whole, z_peer((ma + 1) % GROUP), part_recv.at[c]).wait_recv()
        k = own * ma + size * c
        value = part_send[pl.ds(k, size)]
        for d in range(GROUP - 1):
            value = value + part_all[c, d]
        below = below_all[pl.ds(own * (ma % 2) + size * c, size)]
        new_all[c] = load_in[pl.ds(k, size)] * value / below
        for p in range(GROUP):
            @pl.when(ma != p)
            def _():
                copy(8, new_all.at[c], out_load.at[pl.ds(k, size)], z_peer(p)).start()
    mine = [
        pltpu.make_async_copy(
            new_all.at[c], out_load.at[pl.ds(own * ma + size * c, size)], local_sem.at[4 + c]
        )
        for c in range(CHUNKS)
    ]
    for part in mine:
        part.start()

    for i, (dx, dy) in enumerate(steps):
        @pl.when(exists(dx, dy))
        def _():
            halo(i, dx, dy).wait_send()
            sums(i, dx, dy).wait_send()
    sent(0, xc, xc_peer, gram_a)
    sent(1, ma, z_peer, bg_all)
    sent(2, y, y_peer, gram_b)
    sent(3, xc, xc_peer, prof_1)
    sent(4, y, y_peer, prof_2)
    sent(5, xc, xc_peer, prof_3)
    sent(7, ma, z_peer, gram_c)
    peer = z_peer((ma + 1) % GROUP)
    copy(6, part_all, part_all, peer).wait_send()
    copy_new.wait()
    for part in mine:
        part.wait()
    most = out_load.at[0:nk - own]
    copy(8, most, most, peer).wait_send()
    copy(8, most, most, peer).wait_recv()


def finish(load, prof, out_load, out_prof, sem):
    copies = [pltpu.make_async_copy(load, out_load, sem.at[0]), pltpu.make_async_copy(prof, out_prof, sem.at[1])]
    for c in copies:
        c.start()
    for c in copies:
        c.wait()


def per_device(spectra, loadings, profiles):
    nx, ny, nm = spectra.shape
    nk = loadings.shape[0]
    own = nk // GROUP
    wide_x, wide_y = nx + 2 * RADIUS, ny + 2 * SIDE
    anywhere = pl.BlockSpec(memory_space=pl.ANY)
    vmem = pltpu.VMEM
    held_load, held_prof = pl.pallas_call(
        kernel,
        out_shape=(
            pltpu.VMEM((nk, nx, ny), F32),
            pltpu.VMEM((nk, nm), F32),
        ),
        in_specs=[anywhere] * 3,
        out_specs=(anywhere, anywhere),
        scratch_shapes=[
            vmem((wide_x, wide_y, nm), BF16),
            vmem((nk, nx, ny), F32),
            vmem((nk, nm), F32),
            vmem((wide_x, ny, nm), F32),
            vmem((nx, ny, nm), F32),
            vmem((24, 3 * ny), F32),
            vmem((nx // 2, nk, 2 * ny), F32),
            vmem((nx // 2, 2 * nk, 2 * ny), BF16),
            vmem((nx // 2, 2 * ny, nm), BF16),
            vmem((nx // 2, 2 * ny, nm), BF16),
            vmem((GROUP, nx, ny), F32),
            vmem((GROUP, 8, 128), F32),
            vmem((GROUP, 8, 128), F32),
            vmem((GROUP, 8, 128), F32),
            vmem((GROUP, 8, 128), F32),
            vmem((GROUP, 8, 128), F32),
            vmem((GROUP, 8, 128), F32),
            vmem((nk, nm), F32),
            vmem((GROUP, 8, 128), F32),
            vmem((nk, nx, ny), F32),
            vmem((CHUNKS, GROUP - 1, own // CHUNKS, nx, ny), F32),
            vmem((8, nx, ny), F32),
            vmem((CHUNKS, own // CHUNKS, nx, ny), F32),
            vmem((128, 128), F32),
            vmem((ny, 3 * ny), F32),
            vmem((nx, ny), F32),
            vmem((8, nx, ny), F32),
            vmem((2, 2 * nx, nm), BF16),
            vmem((2, 2 * nx + 32, nm), BF16),
            pltpu.SemaphoreType.DMA((4 + CHUNKS,)),
            pltpu.SemaphoreType.DMA((8,)),
            pltpu.SemaphoreType.DMA((8,)),
            pltpu.SemaphoreType.DMA((8,)),
            pltpu.SemaphoreType.DMA((8,)),
            pltpu.SemaphoreType.DMA((9,)),
            pltpu.SemaphoreType.DMA((9,)),
            pltpu.SemaphoreType.DMA((CHUNKS,)),
            pltpu.SemaphoreType.REGULAR((2,)),
        ],
        compiler_params=pltpu.CompilerParams(
            collective_id=0, has_side_effects=True, vmem_limit_bytes=60 * 1024 * 1024
        ),
    )(spectra, loadings, profiles)
    return pl.pallas_call(
        finish,
        out_shape=(
            jax.ShapeDtypeStruct((nk, nx, ny), F32),
            jax.ShapeDtypeStruct((nk, nm), F32),
        ),
        in_specs=[anywhere] * 2,
        out_specs=(anywhere, anywhere),
        scratch_shapes=[pltpu.SemaphoreType.DMA((2,))],
    )(*(pltpu.with_memory_space_constraint(a, pltpu.VMEM) for a in (held_load, held_prof)))


def solution(mesh):
    return jax.shard_map(
        per_device,
        mesh=mesh,
        in_specs=(P("gx", "gy", "ma"), P(None, "gx", "gy"), P(None, "ma")),
        out_specs=(P(None, "gx", "gy"), P(None, "ma")),
        check_vma=False,
    )
```

```python
import jax
import jax.numpy as jnp
import ml_dtypes
import numpy as np
from jax import lax
from jax.experimental import pallas as pl
from jax.experimental.pallas import tpu as pltpu
from jax.sharding import PartitionSpec as P

MESH = pl.DeviceIdType.MESH
F32 = jnp.float32
BF16 = jnp.bfloat16
HIGH = lax.Precision.HIGHEST

RADIUS = 2
SIDE = 16
GROUP = 8
EPSILON = 1e-06
CHUNKS = 2
ORDER = (4, 3, 5, 2, 6, 1, 7)

NT = (((1,), (1,)), ((), ()))
NN = (((1,), (0,)), ((), ()))


def taps():
    offsets = np.arange(-RADIUS, RADIUS + 1).astype(np.float32)
    raw = np.exp(-offsets * offsets / np.float32(2.0))
    return (raw / np.sum(raw)).astype(np.float32)


def split(value):
    high = value.astype(BF16)
    return high, (value - high.astype(F32)).astype(BF16)


def dot(a, b, dims, precision=None):
    return lax.dot_general(a, b, dims, precision=precision, preferred_element_type=F32)


def band(shape, shift, weights):
    row = lax.broadcasted_iota(jnp.int32, shape, 0)
    column = lax.broadcasted_iota(jnp.int32, shape, 1)
    at = column - row - shift
    out = jnp.zeros(shape, F32)
    for a in range(-RADIUS, RADIUS + 1):
        out = jnp.where(at == a, float(weights[a + RADIUS]), out)
    return out


def block_mask(b):
    lane = lax.broadcasted_iota(jnp.int32, (8, 128), 1)
    return jnp.logical_and(lane >= 32 * b, lane < 32 * (b + 1))


def pack_gram(full):
    out = jnp.zeros((8, 128), F32)
    for b in range(4):
        out = jnp.where(block_mask(b), full[8 * b:8 * b + 8, :], out)
    return out


def unpack_gram(packed):
    return jnp.concatenate([jnp.where(block_mask(b), packed, 0.0) for b in range(4)], axis=0)


def kernel(
    spectra, loadings, profiles, out_load, out_prof,
    ext, load_in, prof_in, ysm, smooth, rows, load_flat, load_split, clean_hi, clean_lo,
    bg_all, gram_a, gram_b, prof_send, prof_1, prof_2, prof_3, prof_new,
    gram_c, part_send, part_all, below_all, new_all, pad_t,
    band_bg, sums_own, sums_in, edge_own, edge_in, local_sem, sums_send, sums_recv, halo_send, halo_recv, send_sem, recv_sem, part_recv, heard,
):
    nx, ny, nm = spectra.shape
    nk = loadings.shape[0]
    size = nk // GROUP // CHUNKS
    own = nk // GROUP
    gx, gy, ma = lax.axis_index("gx"), lax.axis_index("gy"), lax.axis_index("ma")
    count_x, count_y = lax.axis_size("gx"), lax.axis_size("gy")
    half, y = gy // GROUP, gy % GROUP
    xc = gx * 2 + half
    weights = taps()

    def z_peer(p):
        return {"gx": gx, "gy": gy, "ma": p}

    def y_peer(p):
        return {"gx": gx, "gy": half * GROUP + p, "ma": ma}

    def xc_peer(p):
        return {"gx": p // 2, "gy": (p % 2) * GROUP + y, "ma": ma}

    copy_spectra = pltpu.make_async_copy(
        spectra, ext.at[RADIUS:RADIUS + nx, SIDE:SIDE + ny, :], local_sem.at[0]
    )
    copy_load = pltpu.make_async_copy(loadings, load_in, local_sem.at[1])
    copy_prof = pltpu.make_async_copy(profiles, prof_in, local_sem.at[2])
    copy_spectra.start()
    copy_load.start()
    copy_prof.start()

    has = {
        ("x", -1): gx > 0, ("x", 0): None, ("x", 1): gx < count_x - 1,
        ("y", -1): gy > 0, ("y", 0): None, ("y", 1): gy < count_y - 1,
    }
    steps = [(-1, 0), (1, 0), (0, -1), (0, 1), (-1, -1), (-1, 1), (1, -1), (1, 1)]

    def exists(dx, dy):
        a, b = has[("x", dx)], has[("y", dy)]
        if a is None:
            return b
        if b is None:
            return a
        return jnp.logical_and(a, b)

    rows_out = {-1: slice(0, 16), 0: slice(0, 2 * nx), 1: slice(2 * nx - 16, 2 * nx)}
    rows_land = {-1: slice(16 + 2 * nx, 32 + 2 * nx), 0: slice(16, 16 + 2 * nx), 1: slice(0, 16)}
    middle = slice(SIDE, SIDE + ny)

    def halo_refs(dx, dy):
        if dy == 0:
            first, land = (RADIUS, nx + RADIUS) if dx < 0 else (nx, 0)
            return ext.at[first:first + RADIUS, middle, :], ext.at[land:land + RADIUS, middle, :]
        side = (dy + 1) // 2
        return edge_own.at[side, rows_out[dx], :], edge_in.at[1 - side, rows_land[dx], :]

    def halo(i, dx, dy):
        source, target = halo_refs(dx, dy)
        return pltpu.make_async_remote_copy(
            src_ref=source,
            dst_ref=target,
            send_sem=halo_send.at[i],
            recv_sem=halo_recv.at[i],
            device_id={"gx": gx + dx, "gy": gy + dy, "ma": ma},
            device_id_type=MESH,
        )

    barrier = pltpu.get_barrier_semaphore()
    for dx, dy in steps:
        @pl.when(exists(dx, dy))
        def _():
            pl.semaphore_signal(
                barrier, inc=1, device_id={"gx": gx + dx, "gy": gy + dy, "ma": ma}, device_id_type=MESH
            )
    for d in ORDER:
        far = d == GROUP // 2
        near = () if far else (z_peer((ma + d) % GROUP), y_peer((y + d) % GROUP))
        for to in (*near, xc_peer((xc + d) % GROUP)):
            pl.semaphore_signal(barrier, inc=1, device_id=to, device_id_type=MESH)

    copy_spectra.wait()
    ones = jnp.ones((8, nm), BF16)
    for x in range(nx):
        sums_own[x:x + 1, :] = dot(ones, ext[RADIUS + x, SIDE:SIDE + ny, :], NT)[0:1, :]

    hi_taps = weights.astype(ml_dtypes.bfloat16).astype(np.float32)
    lo_taps = (weights - hi_taps).astype(ml_dtypes.bfloat16).astype(np.float32)
    band_bg[...] = band((ny, 3 * ny), ny, hi_taps + lo_taps)

    near_x = (gx > 0).astype(jnp.int32) + (gx < count_x - 1).astype(jnp.int32)
    near_y = (gy > 0).astype(jnp.int32) + (gy < count_y - 1).astype(jnp.int32)
    pl.semaphore_wait(barrier, 3 * (GROUP - 1) - 2 + near_x + near_y + near_x * near_y)

    def sums(i, dx, dy):
        return pltpu.make_async_remote_copy(
            src_ref=sums_own,
            dst_ref=sums_in.at[i],
            send_sem=sums_send.at[i],
            recv_sem=sums_recv.at[i],
            device_id={"gx": gx + dx, "gy": gy + dy, "ma": ma},
            device_id_type=MESH,
        )

    def start(make, chosen):
        for i, (dx, dy) in enumerate(steps):
            if chosen(dy):
                @pl.when(exists(dx, dy))
                def _():
                    make(i, dx, dy).start()

    start(sums, lambda dy: True)
    before_y, before_z = y_peer((y + GROUP - 1) % GROUP), z_peer((ma + GROUP - 1) % GROUP)
    for sem, to in ((0, before_y), (1, before_z)):
        pl.semaphore_signal(heard.at[sem], inc=1, device_id=to, device_id_type=MESH)
    start(halo, lambda dy: dy == 0)
    at = lax.broadcasted_iota(jnp.int32, (2 * nx, 16 * nx), 0)
    column = lax.broadcasted_iota(jnp.int32, (2 * nx, 16 * nx), 1)
    for side, first in ((0, SIDE), (1, SIDE + ny - 16)):
        tile = ext[RADIUS:RADIUS + nx, first:first + 16, :].reshape(16 * nx, nm)
        pick = column == 16 * (at >> 1) + (at & 1) + side * (16 - RADIUS)
        edge_own[side] = dot(jnp.where(pick, 1.0, 0.0).astype(BF16), tile, NN).astype(BF16)
    start(halo, lambda dy: dy != 0)

    def copy(stage, source, target, device, recv=None):
        return pltpu.make_async_remote_copy(
            src_ref=source,
            dst_ref=target,
            send_sem=send_sem.at[stage],
            recv_sem=recv_sem.at[stage] if recv is None else recv,
            device_id=device,
            device_id_type=MESH,
        )

    def exchange(stage, me, peer_id, source, slots):
        for d in ORDER:
            p = (me + d) % GROUP
            copy(stage, source(p), slots.at[me], peer_id(p)).start()

    def arrive(stage, me, peer_id, slots):
        whole = slots.at[0:GROUP - 1]
        copy(stage, whole, whole, peer_id((me + 1) % GROUP)).wait_recv()

    def sent(stage, me, peer_id, slots):
        whole = slots.at[0:GROUP - 1]
        copy(stage, whole, whole, peer_id((me + 1) % GROUP)).wait_send()

    def total(slots):
        out = slots[0]
        for p in range(1, GROUP):
            out = out + slots[p]
        return out

    for dx, dy in steps:
        @pl.when(jnp.logical_not(exists(-dx, -dy)))
        def _():
            unused, target = halo_refs(dx, dy)
            target[...] = jnp.zeros(target.shape, BF16)

    copy_load.wait()
    for x in range(nx):
        load_flat[x // 2, :, 128 * (x % 2):128 * (x % 2) + 128] = load_in[:, x, :]
    full = jnp.zeros((32, 128), F32)
    for i in range(nx // 2):
        part = load_flat[i]
        high, low = split(part)
        load_split[i, 0:32, :] = high
        load_split[i, 32:64, :] = low
        full = full + dot(part, jnp.concatenate([part] * 4, axis=0), NT, HIGH)
    gram_a[xc] = pack_gram(full)
    exchange(0, xc, xc_peer, lambda p: gram_a.at[xc], gram_a)

    for i, (dx, dy) in enumerate(steps):
        there = exists(-dx, -dy)

        @pl.when(there)
        def _():
            sums(i, dx, dy).wait_recv()

        @pl.when(jnp.logical_not(there))
        def _():
            sums_in[i] = jnp.zeros_like(sums_own)
    for side in (-1, 0, 1):
        columns = slice(ny * (side + 1), ny * (side + 2))
        low, high = steps.index((1, -side)), steps.index((-1, -side))
        rows[0:RADIUS, columns] = sums_in[low, nx - RADIUS:nx, :]
        rows[RADIUS:nx + RADIUS, columns] = sums_own[...] if side == 0 else sums_in[steps.index((0, -side))]
        rows[nx + RADIUS:nx + 2 * RADIUS, columns] = sums_in[high, 0:RADIUS, :]

    wide = (ny, ny + 2 * SIDE)
    w0, w1, w2 = (float(weights[RADIUS + a]) for a in range(3))
    row_x = (
        w0 * rows[2:nx + 2, :] + w1 * (rows[1:nx + 1, :] + rows[3:nx + 3, :])
        + w2 * (rows[0:nx, :] + rows[4:nx + 4, :])
    )
    bg_all[ma] = dot(row_x, band_bg[...], NT, HIGH)
    pl.semaphore_wait(heard.at[1], 1)
    exchange(1, ma, z_peer, lambda p: bg_all.at[ma], bg_all)

    arrive(0, xc, xc_peer, gram_a)
    gram_b[y] = total(gram_a)
    pl.semaphore_wait(heard.at[0], 1)
    exchange(2, y, y_peer, lambda p: gram_b.at[y], gram_b)
    band_two = jnp.concatenate(
        [band(wide, SIDE, hi_taps), band(wide, SIDE, lo_taps)], axis=0
    ).astype(BF16)
    for i, (dx, dy) in enumerate(steps):
        @pl.when(exists(-dx, -dy))
        def _():
            halo(i, dx, dy).wait_recv()
    at = lax.broadcasted_iota(jnp.int32, (16 * (nx + 2 * RADIUS), edge_in.shape[1]), 0)
    column = lax.broadcasted_iota(jnp.int32, (16 * (nx + 2 * RADIUS), edge_in.shape[1]), 1)
    for side, first in ((0, SIDE - 16), (1, SIDE + ny)):
        inside = (at & 15) - (16 - RADIUS) * (1 - side)
        pick = jnp.logical_and(
            column == 12 + 2 * (at >> 4) + inside, jnp.logical_and(inside >= 0, inside < RADIUS)
        )
        spread = dot(jnp.where(pick, 1.0, 0.0).astype(BF16), edge_in[side], NN).astype(BF16)
        ext[:, first:first + 16, :] = spread.reshape(nx + 2 * RADIUS, 16, nm)

    @pl.loop(0, (nx + 2 * RADIUS) // 4)
    def _(i):
        for j in range(4):
            x = 4 * i + j
            both = dot(band_two, ext[x], NN)
            ysm[x] = both[0:ny] + both[ny:2 * ny]

    @pl.loop(0, nx // 2)
    def _(i):
        for j in range(2):
            x = 2 * i + j
            smooth[x] = (
                w0 * ysm[x + 2] + w1 * (ysm[x + 1] + ysm[x + 3]) + w2 * (ysm[x] + ysm[x + 4])
            )

    copy_prof.wait()
    arrive(2, y, y_peer, gram_b)
    gram = unpack_gram(total(gram_b))
    old_prof = prof_in[...]
    below_prof = dot(gram, jnp.concatenate([old_prof] * 4, axis=0), NN, HIGH) + EPSILON

    arrive(1, ma, z_peer, bg_all)
    pad_t[0:nx, :] = total(bg_all) * (1.0 / 2048.0)
    back = pad_t[...].T

    acc = jnp.zeros((64, 256), F32)
    acc_lo = jnp.zeros((32, 256), F32)
    for i in range(nx // 2):
        for j in range(2):
            x = 2 * i + j
            value = jnp.maximum(smooth[x] - back[:, x:x + 1], 0.0)
            high, low = split(value)
            clean_hi[i, ny * j:ny * j + ny, :] = high
            clean_lo[i, ny * j:ny * j + ny, :] = low
        acc = acc + dot(load_split[i], clean_hi[i], NN)
        acc_lo = acc_lo + dot(load_split[i, 0:32, :], clean_lo[i], NN)
    numer = acc[0:32] + acc[32:64] + acc_lo

    for p in range(GROUP):
        prof_send[p] = numer[8 * (p // 2):8 * (p // 2) + 8, 128 * (p % 2):128 * (p % 2) + 128]
    exchange(3, xc, xc_peer, lambda p: prof_send.at[p], prof_1)
    prof_1[xc] = prof_send[xc]
    arrive(3, xc, xc_peer, prof_1)
    prof_2[y] = total(prof_1)
    exchange(4, y, y_peer, lambda p: prof_2.at[y], prof_2)
    arrive(4, y, y_peer, prof_2)
    prof_3[xc] = total(prof_2)
    exchange(5, xc, xc_peer, lambda p: prof_3.at[xc], prof_3)
    arrive(5, xc, xc_peer, prof_3)
    numer_prof = jnp.concatenate(
        [jnp.concatenate([prof_3[2 * b], prof_3[2 * b + 1]], axis=1) for b in range(4)], axis=0
    )
    new_prof = old_prof * numer_prof / below_prof

    prof_hi, prof_lo = split(new_prof)
    prof_two = jnp.concatenate([prof_hi, prof_lo], axis=0)
    for i in range(nx // 2):
        both = dot(prof_two, clean_hi[i], NT)
        part = both[0:32] + both[32:64] + dot(prof_hi, clean_lo[i], NT)
        part_send[:, 2 * i, :] = part[:, 0:ny]
        part_send[:, 2 * i + 1, :] = part[:, ny:2 * ny]
    for c in range(CHUNKS):
        for d in ORDER:
            p = (ma + d) % GROUP
            source = part_send.at[pl.ds(own * p + size * c, size)]
            copy(6, source, part_all.at[c, d - 1], z_peer(p), part_recv.at[c]).start()
        if c == 0:
            gram_c[ma] = pack_gram(dot(new_prof, jnp.concatenate([new_prof] * 4, axis=0), NT, HIGH))
            exchange(7, ma, z_peer, lambda p: gram_c.at[ma], gram_c)
    prof_new[...] = new_prof
    copy_new = pltpu.make_async_copy(prof_new, out_prof, local_sem.at[3])
    copy_new.start()

    arrive(7, ma, z_peer, gram_c)
    lane = lax.broadcasted_iota(jnp.int32, (8, 128), 1)
    block = ma // 2
    mask = jnp.logical_and(lane >= 32 * block, lane < 32 * block + 32)
    gram_rows = jnp.where(mask, total(gram_c), 0.0)
    for i in range(nx // 2):
        below = dot(gram_rows, jnp.concatenate([load_flat[i]] * 4, axis=0), NN, HIGH) + EPSILON
        below_all[:, 2 * i, :] = below[:, 0:ny]
        below_all[:, 2 * i + 1, :] = below[:, ny:2 * ny]

    for c in range(CHUNKS):
        whole = part_all.at[c]
        copy(6, whole, whole, z_peer((ma + 1) % GROUP), part_recv.at[c]).wait_recv()
        k = own * ma + size * c
        value = part_send[pl.ds(k, size)]
        for d in range(GROUP - 1):
            value = value + part_all[c, d]
        below = below_all[pl.ds(own * (ma % 2) + size * c, size)]
        new_all[c] = load_in[pl.ds(k, size)] * value / below
        for d in ORDER:
            copy(8, new_all.at[c], out_load.at[pl.ds(k, size)], z_peer((ma + d) % GROUP)).start()
    mine = [
        pltpu.make_async_copy(
            new_all.at[c], out_load.at[pl.ds(own * ma + size * c, size)], local_sem.at[4 + c]
        )
        for c in range(CHUNKS)
    ]
    for part in mine:
        part.start()

    for i, (dx, dy) in enumerate(steps):
        @pl.when(exists(dx, dy))
        def _():
            halo(i, dx, dy).wait_send()
            sums(i, dx, dy).wait_send()
    sent(0, xc, xc_peer, gram_a)
    sent(1, ma, z_peer, bg_all)
    sent(2, y, y_peer, gram_b)
    sent(3, xc, xc_peer, prof_1)
    sent(4, y, y_peer, prof_2)
    sent(5, xc, xc_peer, prof_3)
    sent(7, ma, z_peer, gram_c)
    peer = z_peer((ma + 1) % GROUP)
    copy(6, part_all, part_all, peer).wait_send()
    copy_new.wait()
    for part in mine:
        part.wait()
    most = out_load.at[0:nk - own]
    copy(8, most, most, peer).wait_send()
    copy(8, most, most, peer).wait_recv()


def finish(load, prof, out_load, out_prof, sem):
    copies = [pltpu.make_async_copy(load, out_load, sem.at[0]), pltpu.make_async_copy(prof, out_prof, sem.at[1])]
    for c in copies:
        c.start()
    for c in copies:
        c.wait()


def per_device(spectra, loadings, profiles):
    nx, ny, nm = spectra.shape
    nk = loadings.shape[0]
    own = nk // GROUP
    wide_x, wide_y = nx + 2 * RADIUS, ny + 2 * SIDE
    anywhere = pl.BlockSpec(memory_space=pl.ANY)
    vmem = pltpu.VMEM
    held_load, held_prof = pl.pallas_call(
        kernel,
        out_shape=(
            pltpu.VMEM((nk, nx, ny), F32),
            pltpu.VMEM((nk, nm), F32),
        ),
        in_specs=[anywhere] * 3,
        out_specs=(anywhere, anywhere),
        scratch_shapes=[
            vmem((wide_x, wide_y, nm), BF16),
            vmem((nk, nx, ny), F32),
            vmem((nk, nm), F32),
            vmem((wide_x, ny, nm), F32),
            vmem((nx, ny, nm), F32),
            vmem((24, 3 * ny), F32),
            vmem((nx // 2, nk, 2 * ny), F32),
            vmem((nx // 2, 2 * nk, 2 * ny), BF16),
            vmem((nx // 2, 2 * ny, nm), BF16),
            vmem((nx // 2, 2 * ny, nm), BF16),
            vmem((GROUP, nx, ny), F32),
            vmem((GROUP, 8, 128), F32),
            vmem((GROUP, 8, 128), F32),
            vmem((GROUP, 8, 128), F32),
            vmem((GROUP, 8, 128), F32),
            vmem((GROUP, 8, 128), F32),
            vmem((GROUP, 8, 128), F32),
            vmem((nk, nm), F32),
            vmem((GROUP, 8, 128), F32),
            vmem((nk, nx, ny), F32),
            vmem((CHUNKS, GROUP - 1, own // CHUNKS, nx, ny), F32),
            vmem((8, nx, ny), F32),
            vmem((CHUNKS, own // CHUNKS, nx, ny), F32),
            vmem((128, 128), F32),
            vmem((ny, 3 * ny), F32),
            vmem((nx, ny), F32),
            vmem((8, nx, ny), F32),
            vmem((2, 2 * nx, nm), BF16),
            vmem((2, 2 * nx + 32, nm), BF16),
            pltpu.SemaphoreType.DMA((4 + CHUNKS,)),
            pltpu.SemaphoreType.DMA((8,)),
            pltpu.SemaphoreType.DMA((8,)),
            pltpu.SemaphoreType.DMA((8,)),
            pltpu.SemaphoreType.DMA((8,)),
            pltpu.SemaphoreType.DMA((9,)),
            pltpu.SemaphoreType.DMA((9,)),
            pltpu.SemaphoreType.DMA((CHUNKS,)),
            pltpu.SemaphoreType.REGULAR((2,)),
        ],
        compiler_params=pltpu.CompilerParams(
            collective_id=0, has_side_effects=True, vmem_limit_bytes=60 * 1024 * 1024
        ),
    )(spectra, loadings, profiles)
    return pl.pallas_call(
        finish,
        out_shape=(
            jax.ShapeDtypeStruct((nk, nx, ny), F32),
            jax.ShapeDtypeStruct((nk, nm), F32),
        ),
        in_specs=[anywhere] * 2,
        out_specs=(anywhere, anywhere),
        scratch_shapes=[pltpu.SemaphoreType.DMA((2,))],
    )(*(pltpu.with_memory_space_constraint(a, pltpu.VMEM) for a in (held_load, held_prof)))


def solution(mesh):
    return jax.shard_map(
        per_device,
        mesh=mesh,
        in_specs=(P("gx", "gy", "ma"), P(None, "gx", "gy"), P(None, "ma")),
        out_specs=(P(None, "gx", "gy"), P(None, "ma")),
        check_vma=False,
    )
```

```python
import jax
import jax.numpy as jnp
import ml_dtypes
import numpy as np
from jax import lax
from jax.experimental import pallas as pl
from jax.experimental.pallas import tpu as pltpu
from jax.sharding import PartitionSpec as P

MESH = pl.DeviceIdType.MESH
F32 = jnp.float32
BF16 = jnp.bfloat16
HIGH = lax.Precision.HIGHEST

RADIUS = 2
SIDE = 16
GROUP = 8
EPSILON = 1e-06
CHUNKS = 2
ORDER = (4, 3, 5, 2, 6, 1, 7)

NT = (((1,), (1,)), ((), ()))
NN = (((1,), (0,)), ((), ()))


def taps():
    offsets = np.arange(-RADIUS, RADIUS + 1).astype(np.float32)
    raw = np.exp(-offsets * offsets / np.float32(2.0))
    return (raw / np.sum(raw)).astype(np.float32)


def split(value):
    high = value.astype(BF16)
    return high, (value - high.astype(F32)).astype(BF16)


def dot(a, b, dims, precision=None):
    return lax.dot_general(a, b, dims, precision=precision, preferred_element_type=F32)


def band(shape, shift, weights):
    row = lax.broadcasted_iota(jnp.int32, shape, 0)
    column = lax.broadcasted_iota(jnp.int32, shape, 1)
    at = column - row - shift
    out = jnp.zeros(shape, F32)
    for a in range(-RADIUS, RADIUS + 1):
        out = jnp.where(at == a, float(weights[a + RADIUS]), out)
    return out


def block_mask(b):
    lane = lax.broadcasted_iota(jnp.int32, (8, 128), 1)
    return jnp.logical_and(lane >= 32 * b, lane < 32 * (b + 1))


def pack_gram(full):
    out = jnp.zeros((8, 128), F32)
    for b in range(4):
        out = jnp.where(block_mask(b), full[8 * b:8 * b + 8, :], out)
    return out


def unpack_gram(packed):
    return jnp.concatenate([jnp.where(block_mask(b), packed, 0.0) for b in range(4)], axis=0)


def kernel(
    spectra, loadings, profiles, out_load, out_prof,
    ext, load_in, prof_in, ysm, smooth, rows, load_flat, load_split, clean_hi, clean_lo,
    bg_all, gram_a, gram_b, prof_send, prof_1, prof_2, prof_3, prof_new,
    gram_c, part_send, part_all, below_all, new_all, pad_t,
    band_bg, sums_own, sums_in, edge_own, edge_in, local_sem, sums_send, sums_recv, halo_send, halo_recv, send_sem, recv_sem, part_recv, heard,
):
    nx, ny, nm = spectra.shape
    nk = loadings.shape[0]
    size = nx // CHUNKS
    own = nk // GROUP
    gx, gy, ma = lax.axis_index("gx"), lax.axis_index("gy"), lax.axis_index("ma")
    count_x, count_y = lax.axis_size("gx"), lax.axis_size("gy")
    half, y = gy // GROUP, gy % GROUP
    xc = gx * 2 + half
    weights = taps()

    def z_peer(p):
        return {"gx": gx, "gy": gy, "ma": p}

    def y_peer(p):
        return {"gx": gx, "gy": half * GROUP + p, "ma": ma}

    def xc_peer(p):
        return {"gx": p // 2, "gy": (p % 2) * GROUP + y, "ma": ma}

    copy_spectra = pltpu.make_async_copy(
        spectra, ext.at[RADIUS:RADIUS + nx, SIDE:SIDE + ny, :], local_sem.at[0]
    )
    copy_load = pltpu.make_async_copy(loadings, load_in, local_sem.at[1])
    copy_prof = pltpu.make_async_copy(profiles, prof_in, local_sem.at[2])
    copy_spectra.start()
    copy_load.start()
    copy_prof.start()

    has = {
        ("x", -1): gx > 0, ("x", 0): None, ("x", 1): gx < count_x - 1,
        ("y", -1): gy > 0, ("y", 0): None, ("y", 1): gy < count_y - 1,
    }
    steps = [(-1, 0), (1, 0), (0, -1), (0, 1), (-1, -1), (-1, 1), (1, -1), (1, 1)]

    def exists(dx, dy):
        a, b = has[("x", dx)], has[("y", dy)]
        if a is None:
            return b
        if b is None:
            return a
        return jnp.logical_and(a, b)

    rows_out = {-1: slice(0, 16), 0: slice(0, 2 * nx), 1: slice(2 * nx - 16, 2 * nx)}
    rows_land = {-1: slice(16 + 2 * nx, 32 + 2 * nx), 0: slice(16, 16 + 2 * nx), 1: slice(0, 16)}
    middle = slice(SIDE, SIDE + ny)

    def halo_refs(dx, dy):
        if dy == 0:
            first, land = (RADIUS, nx + RADIUS) if dx < 0 else (nx, 0)
            return ext.at[first:first + RADIUS, middle, :], ext.at[land:land + RADIUS, middle, :]
        side = (dy + 1) // 2
        return edge_own.at[side, rows_out[dx], :], edge_in.at[1 - side, rows_land[dx], :]

    def halo(i, dx, dy):
        source, target = halo_refs(dx, dy)
        return pltpu.make_async_remote_copy(
            src_ref=source,
            dst_ref=target,
            send_sem=halo_send.at[i],
            recv_sem=halo_recv.at[i],
            device_id={"gx": gx + dx, "gy": gy + dy, "ma": ma},
            device_id_type=MESH,
        )

    barrier = pltpu.get_barrier_semaphore()
    for dx, dy in steps:
        @pl.when(exists(dx, dy))
        def _():
            pl.semaphore_signal(
                barrier, inc=1, device_id={"gx": gx + dx, "gy": gy + dy, "ma": ma}, device_id_type=MESH
            )
    for d in ORDER:
        far = d == GROUP // 2
        near = () if far else (z_peer((ma + d) % GROUP), y_peer((y + d) % GROUP))
        for to in (*near, xc_peer((xc + d) % GROUP)):
            pl.semaphore_signal(barrier, inc=1, device_id=to, device_id_type=MESH)

    copy_spectra.wait()
    ones = jnp.ones((8, nm), BF16)
    for x in range(nx):
        sums_own[x:x + 1, :] = dot(ones, ext[RADIUS + x, SIDE:SIDE + ny, :], NT)[0:1, :]

    hi_taps = weights.astype(ml_dtypes.bfloat16).astype(np.float32)
    lo_taps = (weights - hi_taps).astype(ml_dtypes.bfloat16).astype(np.float32)
    band_bg[...] = band((ny, 3 * ny), ny, hi_taps + lo_taps)

    near_x = (gx > 0).astype(jnp.int32) + (gx < count_x - 1).astype(jnp.int32)
    near_y = (gy > 0).astype(jnp.int32) + (gy < count_y - 1).astype(jnp.int32)
    pl.semaphore_wait(barrier, 3 * (GROUP - 1) - 2 + near_x + near_y + near_x * near_y)

    def sums(i, dx, dy):
        return pltpu.make_async_remote_copy(
            src_ref=sums_own,
            dst_ref=sums_in.at[i],
            send_sem=sums_send.at[i],
            recv_sem=sums_recv.at[i],
            device_id={"gx": gx + dx, "gy": gy + dy, "ma": ma},
            device_id_type=MESH,
        )

    def start(make, chosen):
        for i, (dx, dy) in enumerate(steps):
            if chosen(dy):
                @pl.when(exists(dx, dy))
                def _():
                    make(i, dx, dy).start()

    start(sums, lambda dy: True)
    before_y, before_z = y_peer((y + GROUP - 1) % GROUP), z_peer((ma + GROUP - 1) % GROUP)
    for sem, to in ((0, before_y), (1, before_z)):
        pl.semaphore_signal(heard.at[sem], inc=1, device_id=to, device_id_type=MESH)
    start(halo, lambda dy: dy == 0)
    at = lax.broadcasted_iota(jnp.int32, (2 * nx, 16 * nx), 0)
    column = lax.broadcasted_iota(jnp.int32, (2 * nx, 16 * nx), 1)
    for side, first in ((0, SIDE), (1, SIDE + ny - 16)):
        tile = ext[RADIUS:RADIUS + nx, first:first + 16, :].reshape(16 * nx, nm)
        pick = column == 16 * (at >> 1) + (at & 1) + side * (16 - RADIUS)
        edge_own[side] = dot(jnp.where(pick, 1.0, 0.0).astype(BF16), tile, NN).astype(BF16)
    start(halo, lambda dy: dy != 0)

    def copy(stage, source, target, device, recv=None):
        return pltpu.make_async_remote_copy(
            src_ref=source,
            dst_ref=target,
            send_sem=send_sem.at[stage],
            recv_sem=recv_sem.at[stage] if recv is None else recv,
            device_id=device,
            device_id_type=MESH,
        )

    def exchange(stage, me, peer_id, source, slots):
        for d in ORDER:
            p = (me + d) % GROUP
            copy(stage, source(p), slots.at[me], peer_id(p)).start()

    def arrive(stage, me, peer_id, slots):
        whole = slots.at[0:GROUP - 1]
        copy(stage, whole, whole, peer_id((me + 1) % GROUP)).wait_recv()

    def sent(stage, me, peer_id, slots):
        whole = slots.at[0:GROUP - 1]
        copy(stage, whole, whole, peer_id((me + 1) % GROUP)).wait_send()

    def total(slots):
        out = slots[0]
        for p in range(1, GROUP):
            out = out + slots[p]
        return out

    for dx, dy in steps:
        @pl.when(jnp.logical_not(exists(-dx, -dy)))
        def _():
            unused, target = halo_refs(dx, dy)
            target[...] = jnp.zeros(target.shape, BF16)

    copy_load.wait()
    for x in range(nx):
        load_flat[x // 2, :, 128 * (x % 2):128 * (x % 2) + 128] = load_in[:, x, :]
    full = jnp.zeros((32, 128), F32)
    for i in range(nx // 2):
        part = load_flat[i]
        high, low = split(part)
        load_split[i, 0:32, :] = high
        load_split[i, 32:64, :] = low
        full = full + dot(part, jnp.concatenate([part] * 4, axis=0), NT, HIGH)
    gram_a[xc] = pack_gram(full)
    exchange(0, xc, xc_peer, lambda p: gram_a.at[xc], gram_a)

    for i, (dx, dy) in enumerate(steps):
        there = exists(-dx, -dy)

        @pl.when(there)
        def _():
            sums(i, dx, dy).wait_recv()

        @pl.when(jnp.logical_not(there))
        def _():
            sums_in[i] = jnp.zeros_like(sums_own)
    for side in (-1, 0, 1):
        columns = slice(ny * (side + 1), ny * (side + 2))
        low, high = steps.index((1, -side)), steps.index((-1, -side))
        rows[0:RADIUS, columns] = sums_in[low, nx - RADIUS:nx, :]
        rows[RADIUS:nx + RADIUS, columns] = sums_own[...] if side == 0 else sums_in[steps.index((0, -side))]
        rows[nx + RADIUS:nx + 2 * RADIUS, columns] = sums_in[high, 0:RADIUS, :]

    wide = (ny, ny + 2 * SIDE)
    w0, w1, w2 = (float(weights[RADIUS + a]) for a in range(3))
    row_x = (
        w0 * rows[2:nx + 2, :] + w1 * (rows[1:nx + 1, :] + rows[3:nx + 3, :])
        + w2 * (rows[0:nx, :] + rows[4:nx + 4, :])
    )
    bg_all[ma] = dot(row_x, band_bg[...], NT, HIGH)
    pl.semaphore_wait(heard.at[1], 1)
    exchange(1, ma, z_peer, lambda p: bg_all.at[ma], bg_all)

    arrive(0, xc, xc_peer, gram_a)
    gram_b[y] = total(gram_a)
    pl.semaphore_wait(heard.at[0], 1)
    exchange(2, y, y_peer, lambda p: gram_b.at[y], gram_b)
    band_two = jnp.concatenate(
        [band(wide, SIDE, hi_taps), band(wide, SIDE, lo_taps)], axis=0
    ).astype(BF16)
    for i, (dx, dy) in enumerate(steps):
        @pl.when(exists(-dx, -dy))
        def _():
            halo(i, dx, dy).wait_recv()
    at = lax.broadcasted_iota(jnp.int32, (16 * (nx + 2 * RADIUS), edge_in.shape[1]), 0)
    column = lax.broadcasted_iota(jnp.int32, (16 * (nx + 2 * RADIUS), edge_in.shape[1]), 1)
    for side, first in ((0, SIDE - 16), (1, SIDE + ny)):
        inside = (at & 15) - (16 - RADIUS) * (1 - side)
        pick = jnp.logical_and(
            column == 12 + 2 * (at >> 4) + inside, jnp.logical_and(inside >= 0, inside < RADIUS)
        )
        spread = dot(jnp.where(pick, 1.0, 0.0).astype(BF16), edge_in[side], NN).astype(BF16)
        ext[:, first:first + 16, :] = spread.reshape(nx + 2 * RADIUS, 16, nm)

    @pl.loop(0, (nx + 2 * RADIUS) // 4)
    def _(i):
        for j in range(4):
            x = 4 * i + j
            both = dot(band_two, ext[x], NN)
            ysm[x] = both[0:ny] + both[ny:2 * ny]

    @pl.loop(0, nx // 2)
    def _(i):
        for j in range(2):
            x = 2 * i + j
            smooth[x] = (
                w0 * ysm[x + 2] + w1 * (ysm[x + 1] + ysm[x + 3]) + w2 * (ysm[x] + ysm[x + 4])
            )

    copy_prof.wait()
    arrive(2, y, y_peer, gram_b)
    gram = unpack_gram(total(gram_b))
    old_prof = prof_in[...]
    below_prof = dot(gram, jnp.concatenate([old_prof] * 4, axis=0), NN, HIGH) + EPSILON

    arrive(1, ma, z_peer, bg_all)
    pad_t[0:nx, :] = total(bg_all) * (1.0 / 2048.0)
    back = pad_t[...].T

    acc = jnp.zeros((64, 256), F32)
    acc_lo = jnp.zeros((32, 256), F32)
    for i in range(nx // 2):
        for j in range(2):
            x = 2 * i + j
            value = jnp.maximum(smooth[x] - back[:, x:x + 1], 0.0)
            high, low = split(value)
            clean_hi[i, ny * j:ny * j + ny, :] = high
            clean_lo[i, ny * j:ny * j + ny, :] = low
        acc = acc + dot(load_split[i], clean_hi[i], NN)
        acc_lo = acc_lo + dot(load_split[i, 0:32, :], clean_lo[i], NN)
    numer = acc[0:32] + acc[32:64] + acc_lo

    for p in range(GROUP):
        prof_send[p] = numer[8 * (p // 2):8 * (p // 2) + 8, 128 * (p % 2):128 * (p % 2) + 128]
    exchange(3, xc, xc_peer, lambda p: prof_send.at[p], prof_1)
    prof_1[xc] = prof_send[xc]
    arrive(3, xc, xc_peer, prof_1)
    prof_2[y] = total(prof_1)
    exchange(4, y, y_peer, lambda p: prof_2.at[y], prof_2)
    arrive(4, y, y_peer, prof_2)
    prof_3[xc] = total(prof_2)
    exchange(5, xc, xc_peer, lambda p: prof_3.at[xc], prof_3)
    arrive(5, xc, xc_peer, prof_3)
    numer_prof = jnp.concatenate(
        [jnp.concatenate([prof_3[2 * b], prof_3[2 * b + 1]], axis=1) for b in range(4)], axis=0
    )
    new_prof = old_prof * numer_prof / below_prof

    prof_hi, prof_lo = split(new_prof)
    prof_two = jnp.concatenate([prof_hi, prof_lo], axis=0)
    for c in range(CHUNKS):
        for i in range(c * size // 2, (c + 1) * size // 2):
            both = dot(prof_two, clean_hi[i], NT)
            part = both[0:32] + both[32:64] + dot(prof_hi, clean_lo[i], NT)
            part_send[c, :, 2 * i - c * size, :] = part[:, 0:ny]
            part_send[c, :, 2 * i + 1 - c * size, :] = part[:, ny:2 * ny]
        for d in ORDER:
            p = (ma + d) % GROUP
            source = part_send.at[c, pl.ds(own * p, own)]
            copy(6, source, part_all.at[c, d - 1], z_peer(p), part_recv.at[c]).start()
        if c == 0:
            gram_c[ma] = pack_gram(dot(new_prof, jnp.concatenate([new_prof] * 4, axis=0), NT, HIGH))
            exchange(7, ma, z_peer, lambda p: gram_c.at[ma], gram_c)
    prof_new[...] = new_prof
    copy_new = pltpu.make_async_copy(prof_new, out_prof, local_sem.at[3])
    copy_new.start()

    arrive(7, ma, z_peer, gram_c)
    lane = lax.broadcasted_iota(jnp.int32, (8, 128), 1)
    block = ma // 2
    mask = jnp.logical_and(lane >= 32 * block, lane < 32 * block + 32)
    gram_rows = jnp.where(mask, total(gram_c), 0.0)
    for i in range(nx // 2):
        below = dot(gram_rows, jnp.concatenate([load_flat[i]] * 4, axis=0), NN, HIGH) + EPSILON
        below_all[:, 2 * i, :] = below[:, 0:ny]
        below_all[:, 2 * i + 1, :] = below[:, ny:2 * ny]

    for c in range(CHUNKS):
        whole = part_all.at[c]
        copy(6, whole, whole, z_peer((ma + 1) % GROUP), part_recv.at[c]).wait_recv()
        k = own * ma
        band_x = slice(size * c, size * (c + 1))
        value = part_send[c, pl.ds(k, own)]
        for d in range(GROUP - 1):
            value = value + part_all[c, d]
        below = below_all[pl.ds(own * (ma % 2), own), band_x, :]
        new_all[c] = load_in[pl.ds(k, own), band_x, :] * value / below
        for p in range(GROUP):
            @pl.when(ma != p)
            def _():
                copy(8, new_all.at[c], out_load.at[pl.ds(k, own), band_x, :], z_peer(p)).start()
    mine = [
        pltpu.make_async_copy(
            new_all.at[c], out_load.at[pl.ds(own * ma, own), size * c:size * (c + 1), :], local_sem.at[4 + c]
        )
        for c in range(CHUNKS)
    ]
    for part in mine:
        part.start()

    for i, (dx, dy) in enumerate(steps):
        @pl.when(exists(dx, dy))
        def _():
            halo(i, dx, dy).wait_send()
            sums(i, dx, dy).wait_send()
    sent(0, xc, xc_peer, gram_a)
    sent(1, ma, z_peer, bg_all)
    sent(2, y, y_peer, gram_b)
    sent(3, xc, xc_peer, prof_1)
    sent(4, y, y_peer, prof_2)
    sent(5, xc, xc_peer, prof_3)
    sent(7, ma, z_peer, gram_c)
    peer = z_peer((ma + 1) % GROUP)
    copy(6, part_all, part_all, peer).wait_send()
    copy_new.wait()
    for part in mine:
        part.wait()
    most = out_load.at[0:nk - own]
    copy(8, most, most, peer).wait_send()
    copy(8, most, most, peer).wait_recv()


def finish(load, prof, out_load, out_prof, sem):
    copies = [pltpu.make_async_copy(load, out_load, sem.at[0]), pltpu.make_async_copy(prof, out_prof, sem.at[1])]
    for c in copies:
        c.start()
    for c in copies:
        c.wait()


def per_device(spectra, loadings, profiles):
    nx, ny, nm = spectra.shape
    nk = loadings.shape[0]
    own = nk // GROUP
    wide_x, wide_y = nx + 2 * RADIUS, ny + 2 * SIDE
    anywhere = pl.BlockSpec(memory_space=pl.ANY)
    vmem = pltpu.VMEM
    held_load, held_prof = pl.pallas_call(
        kernel,
        out_shape=(
            pltpu.VMEM((nk, nx, ny), F32),
            pltpu.VMEM((nk, nm), F32),
        ),
        in_specs=[anywhere] * 3,
        out_specs=(anywhere, anywhere),
        scratch_shapes=[
            vmem((wide_x, wide_y, nm), BF16),
            vmem((nk, nx, ny), F32),
            vmem((nk, nm), F32),
            vmem((wide_x, ny, nm), F32),
            vmem((nx, ny, nm), F32),
            vmem((24, 3 * ny), F32),
            vmem((nx // 2, nk, 2 * ny), F32),
            vmem((nx // 2, 2 * nk, 2 * ny), BF16),
            vmem((nx // 2, 2 * ny, nm), BF16),
            vmem((nx // 2, 2 * ny, nm), BF16),
            vmem((GROUP, nx, ny), F32),
            vmem((GROUP, 8, 128), F32),
            vmem((GROUP, 8, 128), F32),
            vmem((GROUP, 8, 128), F32),
            vmem((GROUP, 8, 128), F32),
            vmem((GROUP, 8, 128), F32),
            vmem((GROUP, 8, 128), F32),
            vmem((nk, nm), F32),
            vmem((GROUP, 8, 128), F32),
            vmem((CHUNKS, nk, nx // CHUNKS, ny), F32),
            vmem((CHUNKS, GROUP - 1, own, nx // CHUNKS, ny), F32),
            vmem((8, nx, ny), F32),
            vmem((CHUNKS, own, nx // CHUNKS, ny), F32),
            vmem((128, 128), F32),
            vmem((ny, 3 * ny), F32),
            vmem((nx, ny), F32),
            vmem((8, nx, ny), F32),
            vmem((2, 2 * nx, nm), BF16),
            vmem((2, 2 * nx + 32, nm), BF16),
            pltpu.SemaphoreType.DMA((4 + CHUNKS,)),
            pltpu.SemaphoreType.DMA((8,)),
            pltpu.SemaphoreType.DMA((8,)),
            pltpu.SemaphoreType.DMA((8,)),
            pltpu.SemaphoreType.DMA((8,)),
            pltpu.SemaphoreType.DMA((9,)),
            pltpu.SemaphoreType.DMA((9,)),
            pltpu.SemaphoreType.DMA((CHUNKS,)),
            pltpu.SemaphoreType.REGULAR((2,)),
        ],
        compiler_params=pltpu.CompilerParams(
            collective_id=0, has_side_effects=True, vmem_limit_bytes=60 * 1024 * 1024
        ),
    )(spectra, loadings, profiles)
    return pl.pallas_call(
        finish,
        out_shape=(
            jax.ShapeDtypeStruct((nk, nx, ny), F32),
            jax.ShapeDtypeStruct((nk, nm), F32),
        ),
        in_specs=[anywhere] * 2,
        out_specs=(anywhere, anywhere),
        scratch_shapes=[pltpu.SemaphoreType.DMA((2,))],
    )(*(pltpu.with_memory_space_constraint(a, pltpu.VMEM) for a in (held_load, held_prof)))


def solution(mesh):
    return jax.shard_map(
        per_device,
        mesh=mesh,
        in_specs=(P("gx", "gy", "ma"), P(None, "gx", "gy"), P(None, "ma")),
        out_specs=(P(None, "gx", "gy"), P(None, "ma")),
        check_vma=False,
    )
```
